32 devices in a mesh: space: 8 (over z, y), field: 4 (over x, core).
Axes of the slice: x: 2, y: 2, z: 4, core: 2. Of those that a mesh axis runs over, the one named last changes fastest.
Arguments:
- fields: float32 [16, 256, 6144], P('field', 'space'), may hold values from -6 to 6
- zone_ids: int32 [256, 6144], P('space'), may hold values from 0 to 7
- diffusivity: float32 [16, 8], P('field'), may hold values from 0.3 to 3
- heat_rate: float32 [15], replicated, may hold values from 0.3 to 1.5
- weight_in: bfloat16 [384, 16], replicated, may hold values from -1.5 to 1.5
- bias_in: float32 [384], replicated, may hold values from -3 to 3
- weight_mid: bfloat16 [384, 384], replicated, may hold values from -0.3125 to 0.3125
- bias_mid: float32 [384], replicated, may hold values from -3 to 3
- weight_out: bfloat16 [16, 384], replicated, may hold values from -0.3125 to 0.3125
- bias_out: float32 [16], replicated, may hold values from -2 to 2
Outputs:
- new_fields: float32 [16, 256, 6144], P('field', 'space')
The draws below stay inside these ranges and needn't reach their ends.
All inputs are finite; a program needn't handle non-finite values.
Results may differ from the reference program's by a relative error of at most 0.005.
Values may be sent and summed in bfloat16 or wider, within the bound.
A program may use at most 64 MiB of HBM per device.

```python
import math
import jax
import jax.numpy as jnp
from jax import lax

FIELDS = 16
COMPS = 15
HID = 384
ZONES = 8
SWEEPS = 3
ROWS_BLK = 1024
NY = 6144
NX = 256


def set_ends(values, key, smallest, high):
    dims = values.shape
    index_at = [jax.random.randint(jax.random.fold_in(key, axis), (), 0, dims[axis]) for axis in range(len(dims))]
    values = values.at[tuple(index_at)].set(smallest)
    longest = dims.index(max(dims))
    index_at[longest] = (index_at[longest] + 1) % dims[longest]
    return values.at[tuple(index_at)].set(high)


def shard_levels(own_key, extent, shards, smallest, largest):
    level, own = 1.0, jax.random.fold_in(own_key, 6)
    for axis_at, blocks in shards:
        draws = jnp.exp(jax.random.uniform(jax.random.fold_in(own, axis_at), (blocks,), jnp.float32, smallest / len(shards), largest / len(shards)))
        level = level * jnp.repeat(draws, extent[axis_at] // blocks).reshape([-1 if axis == axis_at else 1 for axis in range(len(extent))])
    return level


def noise(own_key, dims, scale, reach, split=(), kind=jnp.bfloat16):
    values = jax.random.normal(own_key, dims, jnp.float32) * scale
    if len(split) > 0:
        values = shard_levels(own_key, dims, split, -0.22, 0.18) * values
    return jnp.clip(values, min=-reach, max=reach).astype(kind)


def setup_inputs(seed: int = 0) -> dict:
    arg_keys = jax.random.split(jax.random.key(seed), 11)
    fields = noise(arg_keys[0], (FIELDS, NX, NY), 1.0, 6.0, ((0, 4), (1, 8)), jnp.float32)
    zone_ids = set_ends(jax.random.randint(arg_keys[1], (NX, NY), 0, ZONES), jax.random.fold_in(arg_keys[1], 1), 0, ZONES - 1).astype(jnp.int32)
    diffusivity = jnp.clip(jnp.exp(math.log(3.0) - 2.3025851 * jax.random.uniform(arg_keys[2], (FIELDS, ZONES), jnp.float32) ** shard_levels(arg_keys[2], (FIELDS, ZONES), ((0, 4),), -0.2, 0.2)), 0.3, 3.0)
    heat_rate = jnp.clip(jnp.exp(jax.random.uniform(arg_keys[3], (COMPS,), jnp.float32, math.log(0.3), math.log(1.5))), 0.3, 1.5)
    weight_in = noise(arg_keys[4], (HID, FIELDS), FIELDS ** -0.5, 1.5)
    bias_in = noise(arg_keys[5], (HID,), 0.5, 3.0, (), jnp.float32)
    weight_mid = noise(arg_keys[6], (HID, HID), HID ** -0.5, 0.3125)
    bias_mid = noise(arg_keys[7], (HID,), 0.5, 3.0, (), jnp.float32)
    weight_out = noise(arg_keys[8], (FIELDS, HID), HID ** -0.5, 0.3125)
    bias_out = noise(arg_keys[9], (FIELDS,), 0.3, 2.0, (), jnp.float32)
    return {"fields": fields, "zone_ids": zone_ids, "diffusivity": diffusivity, "heat_rate": heat_rate, "weight_in": weight_in, "bias_in": bias_in, "weight_mid": weight_mid, "bias_mid": bias_mid, "weight_out": weight_out, "bias_out": bias_out}


RELAX_WEIGHTS = (0.8, 1.25, 0.95)


def relax_step(padded, source, coef_pad, weight):
    middle = padded[:, 1:-1]
    coef_mid = coef_pad[:, 1:-1]
    face_north = 0.5 * (coef_mid + coef_pad[:, 2:])
    face_south = 0.5 * (coef_mid + coef_pad[:, :-2])
    face_east = 0.5 * (coef_mid + jnp.roll(coef_mid, -1, 2))
    face_west = 0.5 * (coef_mid + jnp.roll(coef_mid, 1, 2))
    diagonal = 1.0 + face_north + face_south + face_east + face_west
    image = diagonal * middle - face_north * padded[:, 2:] - face_south * padded[:, :-2]
    image = image - face_east * jnp.roll(middle, -1, 2) - face_west * jnp.roll(middle, 1, 2)
    return middle + weight * (source - image) / diagonal


def lookup(zone_ids, diffusivity):
    coefs = jnp.zeros((diffusivity.shape[0],) + zone_ids.shape, jnp.float32)
    for number in range(diffusivity.shape[1]):
        coefs = coefs + jnp.where((zone_ids == number)[None], diffusivity[:, number][:, None, None], jnp.float32(0.0))
    return coefs


def surrogate(inputs, weight_in, bias_in, weight_mid, bias_mid, weight_out, bias_out):
    hidden = jax.nn.silu(jnp.dot(weight_in, inputs, preferred_element_type=jnp.float32) + bias_in[:, None]).astype(jnp.bfloat16)
    hidden = jax.nn.silu(jnp.dot(weight_mid, hidden, preferred_element_type=jnp.float32) + bias_mid[:, None]).astype(jnp.bfloat16)
    return (jnp.dot(weight_out, hidden, preferred_element_type=jnp.float32) + bias_out[:, None]).astype(jnp.bfloat16)


def pad_rows(array):
    return jnp.pad(array, ((0, 0), (1, 1), (0, 0)))


def reference(fields, zone_ids, diffusivity, heat_rate, weight_in, bias_in, weight_mid, bias_mid, weight_out, bias_out):
    coefs = lookup(zone_ids, diffusivity)
    coef_pad = pad_rows(coefs)
    state = fields
    for number in range(SWEEPS):
        state = relax_step(pad_rows(state), fields, coef_pad, RELAX_WEIGHTS[number])
    cells = NX * NY
    by_block = state.astype(jnp.bfloat16).reshape(FIELDS, cells // ROWS_BLK, ROWS_BLK).transpose(1, 0, 2)

    def apply_block(row_block):
        return surrogate(row_block, weight_in, bias_in, weight_mid, bias_mid, weight_out, bias_out)

    change = lax.map(apply_block, by_block).transpose(1, 0, 2).reshape(FIELDS, NX, NY).astype(jnp.float32)
    new_heat = state[-1] + change[-1]
    factor = jnp.exp(heat_rate[:, None, None] * jnp.tanh(new_heat)[None])
    scaled = (change[:-1] * factor).astype(jnp.bfloat16).astype(jnp.float32)
    species = state[:-1] + scaled
    return jnp.concatenate([species, new_heat[None]], 0)
```

```python
import functools

import jax
import jax.numpy as jnp
from jax import lax
from jax.experimental import pallas as pl
from jax.experimental.pallas import tpu as pltpu
from jax.sharding import PartitionSpec as P

FIELDS = 16
SWEEPS = 3
HALO = 3
SUB = 8
PAIR = 16
LANES = 256
STEP = 256
RELAX_WEIGHTS = (0.8, 1.25, 0.95)
MESH = pl.DeviceIdType.MESH
F32 = jnp.float32
BF16 = jnp.bfloat16


def iota2(shape, axis):
    return lax.broadcasted_iota(jnp.int32, shape, axis)


def three_rows(row):
    high = row.astype(BF16).astype(F32)
    rest = row - high
    mid = rest.astype(BF16).astype(F32)
    low = rest - mid
    index = iota2((PAIR, row.shape[1]), 0)
    zero = jnp.zeros((PAIR, row.shape[1]), F32)
    out = jnp.where(index == 0, high, zero)
    out = jnp.where(index == 1, mid, out)
    out = jnp.where(index == 2, low, out)
    return out.astype(BF16)


def across(rows16, select):
    return lax.dot_general(rows16, select, (((0,), (0,)), ((), ())), preferred_element_type=F32)


def halves_silu(pre):
    y = pre.astype(BF16)
    return y + y * jnp.tanh(y)


def kernel(
    n,
    n_space,
    fields,
    zones,
    diff,
    rate,
    w_in,
    b_in,
    w_mid,
    b_mid,
    w_out,
    b_out,
    out,
    src,
    coef,
    face_d,
    face_e,
    rdiag,
    s1,
    s2,
    s3,
    halo_out,
    halo_in,
    sbuf,
    xbuf,
    rbuf,
    ret,
    w1,
    w2,
    w3,
    rate_row,
    rate_col,
    halo_ssem,
    halo_rsem,
    ssem,
    rsem,
    rssem,
    rrsem,
    lsem,
    rlsem,
):
    per, rows, columns = fields.shape
    parts = SUB // per
    width = columns // parts
    variants = 2 * parts
    hid = w_mid.shape[0]
    chunks = rows // (2 * n)
    chunk_rows = rows // chunks
    groups = rows // SUB
    here = lax.axis_index("space")
    me = lax.axis_index("field")
    has_up = here > 0
    has_down = here < n_space - 1

    barrier = pltpu.get_barrier_semaphore()
    for off in range(1, n):
        pl.semaphore_signal(
            barrier, inc=1, device_id={"field": lax.rem(me + off, n)}, device_id_type=MESH
        )

    @pl.when(has_up)
    def _():
        pl.semaphore_signal(barrier, inc=1, device_id={"space": here - 1}, device_id_type=MESH)

    @pl.when(has_down)
    def _():
        pl.semaphore_signal(barrier, inc=1, device_id={"space": here + 1}, device_id_type=MESH)

    def prep(g):
        row0 = pl.multiple_of(g * SUB, SUB)
        there = pl.ds(pl.multiple_of((row0 + HALO) * SUB, SUB), SUB * SUB)

        def lane_block(j, carry):
            at = pl.multiple_of(j * STEP, STEP)
            coefs, values = [], []
            for p in range(parts):
                cols = pl.ds(pl.multiple_of(at + p * width, STEP), STEP)
                zone = zones[pl.ds(row0, SUB), cols]
                for f in range(per):
                    value = jnp.full(zone.shape, diff[f, 0], F32)
                    for z in range(1, diff.shape[1]):
                        value = jnp.where(zone == z, diff[f, z], value)
                    coefs.append(value)
                    values.append(fields[f, pl.ds(row0, SUB), cols])
            for buf, made in ((coef, coefs), (src, values)):
                turned = jnp.swapaxes(jnp.stack(made, 0), 0, 1)
                buf[there, pl.ds(at, STEP)] = turned.reshape(SUB * SUB, STEP)
            return carry

        lax.fori_loop(0, width // STEP, lane_block, 0)

    def prep_end(i, carry):
        prep(i * (groups - 1))
        return carry

    lax.fori_loop(0, 2, prep_end, 0)
    top = HALO * SUB
    for side, row in ((0, HALO), (1, rows)):
        halo_out[side] = jnp.concatenate(
            [src[row * SUB : row * SUB + top, :], coef[row * SUB : row * SUB + top, :]], 0
        ).astype(BF16)
    heard = (n - 1) + has_up.astype(jnp.int32) + has_down.astype(jnp.int32)
    pl.semaphore_wait(barrier, heard)

    def halo_copy(side):
        target = here - 1 if side == 0 else here + 1
        return pltpu.make_async_remote_copy(
            src_ref=halo_out.at[side],
            dst_ref=halo_in.at[1 - side],
            send_sem=halo_ssem.at[side],
            recv_sem=halo_rsem.at[1 - side],
            device_id={"space": target},
            device_id_type=MESH,
        )

    @pl.when(has_up)
    def _():
        halo_copy(0).start()

    @pl.when(has_down)
    def _():
        halo_copy(1).start()

    def prep_mid(g, carry):
        prep(g)
        return carry

    lax.fori_loop(1, groups - 1, prep_mid, 0)

    lane0 = iota2((SUB, 128), 1) == 0
    lane_last = iota2((SUB, 128), 1) == 127

    def from_east(x):
        rolled = pltpu.roll(x, width - 1, 1)
        tail = rolled[:, width - 128 :]
        tail = jnp.where(lane_last, pltpu.roll(tail, SUB - per, 0), tail)
        return jnp.concatenate([rolled[:, : width - 128], tail], 1)

    def from_west(x):
        rolled = pltpu.roll(x, 1, 1)
        head = rolled[:, :128]
        head = jnp.where(lane0, pltpu.roll(head, per, 0), head)
        return jnp.concatenate([head, rolled[:, 128:]], 1)

    def at_row(r):
        return pl.ds(pl.multiple_of(r * SUB, SUB), SUB)

    def first_row(r, carry):
        a, b, c = at_row(r - 1), at_row(r), at_row(r + 1)
        mine = coef[b, :]
        down = 0.5 * (mine + coef[c, :])
        up = 0.5 * (mine + coef[a, :])
        east = 0.5 * (mine + from_east(mine))
        west = from_west(east)
        outside = jnp.logical_or(
            jnp.logical_and(r < HALO, jnp.logical_not(has_up)),
            jnp.logical_and(r >= rows + HALO, jnp.logical_not(has_down)),
        )
        scale = jnp.where(outside, 0.0, 1.0).astype(F32)
        inv = scale / (1.0 + down + up + east + west)
        face_d[b, :] = down
        face_e[b, :] = east
        rdiag[b, :] = inv
        v = src[b, :]
        total = v + down * src[c, :] + up * src[a, :]
        total = total + east * from_east(v) + from_west(east * v)
        weight = RELAX_WEIGHTS[0]
        s1[b, :] = (1.0 - weight) * v + (weight * inv) * total
        return carry

    def later_row(old, new, weight, r, carry):
        a, b, c = at_row(r - 1), at_row(r), at_row(r + 1)
        v = old[b, :]
        east = face_e[b, :]
        total = src[b, :] + face_d[b, :] * old[c, :] + face_d[a, :] * old[a, :]
        total = total + east * from_east(v) + from_west(east * v)
        new[b, :] = (1.0 - weight) * v + (weight * rdiag[b, :]) * total
        return carry

    steps = (
        first_row,
        functools.partial(later_row, s1, s2, RELAX_WEIGHTS[1]),
        functools.partial(later_row, s2, s3, RELAX_WEIGHTS[2]),
    )
    done = [set() for _ in steps]

    def stencil(k):
        low, high = k * chunk_rows + HALO, (k + 1) * chunk_rows + HALO
        for number, step in enumerate(steps):
            grow = SWEEPS - 1 - number
            need = sorted(set(range(low - grow, high + grow)) - done[number])
            done[number].update(need)
            lax.fori_loop(need[0], need[-1] + 1, step, 0)
        for d in range(n):
            row = (low + 2 * d) * SUB
            sbuf[k, d] = s3[row : row + PAIR, :].astype(BF16)
        for c in sends(k):
            c.start()

    def all_copies(src_buf, dst_buf, k, send_sem, recv_sem, local_sem):
        copies = []
        for off in range(1, n):
            peer = lax.rem(me + off, n)
            copies.append(
                pltpu.make_async_remote_copy(
                    src_ref=src_buf.at[k, peer],
                    dst_ref=dst_buf.at[k, me],
                    send_sem=send_sem.at[k, off],
                    recv_sem=recv_sem.at[k, off],
                    device_id={"field": peer},
                    device_id_type=MESH,
                )
            )
        local = pltpu.make_async_copy(src_buf.at[k, me], dst_buf.at[k, me], local_sem.at[k])
        return copies + [local]

    def sends(k):
        return all_copies(sbuf, xbuf, k, ssem, rsem, lsem)

    def returns(k):
        return all_copies(rbuf, ret, k, rssem, rrsem, rlsem)

    def halo_wait():
        for slot, row, has in ((0, 0, has_up), (1, rows + HALO, has_down)):
            there = pl.ds(row * SUB, top)

            @pl.when(has)
            def _():
                copy = halo_copy(1 - slot)
                copy.wait_recv()
                both = halo_in[slot].astype(F32)
                src[there, :] = both[:top]
                coef[there, :] = both[top:]

            @pl.when(jnp.logical_not(has))
            def _():
                src[there, :] = jnp.zeros((top, width), F32)
                coef[there, :] = jnp.zeros((top, width), F32)

        @pl.when(has_up)
        def _():
            halo_copy(0).wait_send()

        @pl.when(has_down)
        def _():
            halo_copy(1).wait_send()

    def weights():
        depth = (n + 1) * PAIR
        bias = three_rows(0.5 * b_in[...])
        row, col = iota2((PAIR, depth), 0), iota2((PAIR, depth), 1)
        bias_cols = across(bias, (col == row + n * PAIR).astype(BF16))
        for v in range(variants):
            place = (row // per) * PAIR + v * per + lax.rem(row, per)
            pick = jnp.where(col == place, 0.5, 0.0).astype(BF16)
            spread = jnp.dot(w_in[...], pick, preferred_element_type=F32)
            w1[v * hid : (v + 1) * hid, :] = (spread + bias_cols).astype(BF16)
        square = (iota2((PAIR, PAIR), 0) == iota2((PAIR, PAIR), 1)).astype(BF16)
        w2[:, :hid] = w_mid[...] * jnp.asarray(0.5, BF16)
        w2[:, hid:] = across(three_rows(0.5 * b_mid[...]), square).astype(BF16)
        w3[:, :hid] = w_out[...]
        w3[:, hid:] = across(three_rows(b_out[...]), square).astype(BF16)
        rate_row[...] = jnp.zeros(rate_row.shape, F32)
        rate_row[0:1, 0 : FIELDS - 1] = rate[...]
        ones = jnp.ones((PAIR, LANES), BF16)
        rate_col[...] = across(three_rows(rate_row[0:1, :])[:, :FIELDS], ones)
        for k in range(chunks):
            xbuf[k, n] = jnp.ones((PAIR, width), BF16)

    def surrogate(k):
        ones = jnp.ones((PAIR, LANES), BF16)
        for c in sends(k):
            c.wait()

        def block(j, carry):
            lanes = pl.ds(pl.multiple_of(j * LANES, LANES), LANES)
            x = xbuf[k, :, :, lanes].reshape((n + 1) * PAIR, LANES)
            heat_in = xbuf[k, n - 1, :, lanes].astype(F32)
            scaled = []
            for v in range(variants):
                pre = jnp.dot(w1[v * hid : (v + 1) * hid, :], x, preferred_element_type=F32)
                hidden = jnp.concatenate([halves_silu(pre), ones], 0)
                pre = jnp.dot(w2[...], hidden, preferred_element_type=F32)
                hidden = jnp.concatenate([halves_silu(pre), ones], 0)
                change = jnp.dot(w3[...], hidden, preferred_element_type=F32)
                last = v * per + per - 1
                heat = heat_in[last : last + 1] + change[FIELDS - 1 :]
                scaled.append(change * jnp.exp(rate_col[...] * jnp.tanh(heat)))
            for s in range(n):
                block_out = jnp.concatenate([one[s * per : (s + 1) * per] for one in scaled], 0)
                rbuf[k, s, :, lanes] = block_out.astype(BF16)
            return carry

        lax.fori_loop(0, width // LANES, block, 0)
        for c in returns(k):
            c.start()

    def finish(k):
        for c in returns(k):
            c.wait()
        low = k * chunk_rows + HALO
        for d in range(n):
            row = (low + 2 * d) * SUB
            s3[row : row + PAIR, :] = s3[row : row + PAIR, :] + ret[k, d].astype(F32)
        for g in range(k * chunk_rows // SUB, (k + 1) * chunk_rows // SUB):

            def lane_block(j, carry, g=g):
                at = pl.multiple_of(j * STEP, STEP)
                slab = s3[(g * SUB + HALO) * SUB : ((g + 1) * SUB + HALO) * SUB, pl.ds(at, STEP)]
                turned = jnp.swapaxes(slab.reshape(SUB, SUB, STEP), 0, 1)
                for p in range(parts):
                    cols = pl.ds(pl.multiple_of(at + p * width, STEP), STEP)
                    for f in range(per):
                        out[f, pl.ds(g * SUB, SUB), cols] = turned[p * per + f]
                return carry

            lax.fori_loop(0, width // STEP, lane_block, 0)

    inner = list(range(1, chunks - 1))
    edge = [k for k in range(chunks) if k not in inner]
    for k in inner:
        stencil(k)
    weights()
    order = inner + edge
    begun = 0
    if inner:
        surrogate(order[0])
        begun = 1
    halo_wait()
    for k in edge:
        stencil(k)
    for i in range(begun, chunks):
        surrogate(order[i])
        if i > 0:
            finish(order[i - 1])
    finish(order[-1])


def on_device(
    n,
    n_space,
    fields,
    zone_ids,
    diffusivity,
    heat_rate,
    weight_in,
    bias_in,
    weight_mid,
    bias_mid,
    weight_out,
    bias_out,
):
    per, rows, columns = fields.shape
    width = columns * per // SUB
    variants = 2 * SUB // per
    hid = weight_mid.shape[0]
    chunks = rows // (2 * n)
    padded = (rows + 2 * HALO) * SUB
    vmem = pl.BlockSpec(memory_space=pltpu.VMEM)
    smem = pl.BlockSpec(memory_space=pltpu.SMEM)
    slab = pltpu.VMEM((padded, width), F32)
    dma = pltpu.SemaphoreType.DMA
    return pl.pallas_call(
        functools.partial(kernel, n, n_space),
        out_shape=jax.ShapeDtypeStruct(fields.shape, F32),
        in_specs=[vmem, vmem, smem] + [vmem] * 7,
        out_specs=vmem,
        scratch_shapes=[slab] * 8
        + [
            pltpu.VMEM((2, 2 * HALO * SUB, width), BF16),
            pltpu.VMEM((2, 2 * HALO * SUB, width), BF16),
            pltpu.VMEM((chunks, n, PAIR, width), BF16),
            pltpu.VMEM((chunks, n + 1, PAIR, width), BF16),
            pltpu.VMEM((chunks, n, PAIR, width), BF16),
            pltpu.VMEM((chunks, n, PAIR, width), BF16),
            pltpu.VMEM((variants * hid, (n + 1) * PAIR), BF16),
            pltpu.VMEM((hid, hid + PAIR), BF16),
            pltpu.VMEM((FIELDS, hid + PAIR), BF16),
            pltpu.VMEM((SUB, 128), F32),
            pltpu.VMEM((FIELDS, LANES), F32),
            dma((2,)),
            dma((2,)),
            dma((chunks, n)),
            dma((chunks, n)),
            dma((chunks, n)),
            dma((chunks, n)),
            dma((chunks,)),
            dma((chunks,)),
        ],
        compiler_params=pltpu.CompilerParams(
            collective_id=0, has_side_effects=True, vmem_limit_bytes=60 * 1024 * 1024
        ),
        cost_estimate=pl.CostEstimate(
            flops=2 * per * rows * columns // n * hid * (hid + 2 * FIELDS),
            bytes_accessed=9 * per * rows * columns,
            transcendentals=0,
        ),
    )(
        fields,
        zone_ids,
        diffusivity,
        heat_rate[None],
        weight_in,
        bias_in[None],
        weight_mid,
        bias_mid[None],
        weight_out,
        bias_out[None],
    )


def solution(mesh):
    n, n_space = mesh.shape["field"], mesh.shape["space"]
    return jax.shard_map(
        functools.partial(on_device, n, n_space),
        mesh=mesh,
        in_specs=(
            P("field", "space", None),
            P("space", None),
            P("field", None),
            P(),
            P(),
            P(),
            P(),
            P(),
            P(),
            P(),
        ),
        out_specs=P("field", "space", None),
        check_vma=False,
    )
```

```python
import functools

import jax
import jax.numpy as jnp
from jax import lax
from jax.experimental import pallas as pl
from jax.experimental.pallas import tpu as pltpu
from jax.sharding import PartitionSpec as P

FIELDS = 16
SWEEPS = 3
HALO = 3
SUB = 8
PAIR = 16
STEP = 256
RELAX_WEIGHTS = (0.8, 1.25, 0.95)
MESH = pl.DeviceIdType.MESH
F32 = jnp.float32
BF16 = jnp.bfloat16


def block_lanes(width):
    return 512 if width % 512 == 0 else 256


def iota2(shape, axis):
    return lax.broadcasted_iota(jnp.int32, shape, axis)


def three_rows(row):
    row = row.reshape(1, -1)
    high = row.astype(BF16).astype(F32)
    rest = row - high
    mid = rest.astype(BF16).astype(F32)
    low = rest - mid
    index = iota2((PAIR, row.shape[1]), 0)
    zero = jnp.zeros((PAIR, row.shape[1]), F32)
    out = jnp.where(index == 0, high, zero)
    out = jnp.where(index == 1, mid, out)
    out = jnp.where(index == 2, low, out)
    return out.astype(BF16)


def across(rows16, select):
    return lax.dot_general(rows16, select, (((0,), (0,)), ((), ())), preferred_element_type=F32)


def halves_silu(pre):
    y = pre.astype(BF16)
    return y + y * jnp.tanh(y)


def kernel(
    n,
    n_space,
    fields,
    zones,
    diff,
    rate,
    w_in,
    b_in,
    w_mid,
    b_mid,
    w_out,
    b_out,
    out,
    src,
    coef,
    face_d,
    face_e,
    rdiag,
    s1,
    s2,
    s3,
    halo_out,
    halo_in,
    sbuf,
    xbuf,
    rbuf,
    ret,
    w1,
    w2,
    w3,
    rate_row,
    rate_col,
    halo_ssem,
    halo_rsem,
    ssem,
    rsem,
    rssem,
    rrsem,
    lsem,
    rlsem,
):
    per, rows, columns = fields.shape
    parts = SUB // per
    width = columns // parts
    variants = 2 * parts
    lanes_at_once = block_lanes(width)
    hid = w_mid.shape[0]
    chunks = rows // (2 * n)
    chunk_rows = rows // chunks
    groups = rows // SUB
    here = lax.axis_index("space")
    me = lax.axis_index("field")
    has_up = here > 0
    has_down = here < n_space - 1

    barrier = pltpu.get_barrier_semaphore()
    for off in range(1, n):
        pl.semaphore_signal(
            barrier, inc=1, device_id={"field": lax.rem(me + off, n)}, device_id_type=MESH
        )

    @pl.when(has_up)
    def _():
        pl.semaphore_signal(barrier, inc=1, device_id={"space": here - 1}, device_id_type=MESH)

    @pl.when(has_down)
    def _():
        pl.semaphore_signal(barrier, inc=1, device_id={"space": here + 1}, device_id_type=MESH)

    def prep(g):
        row0 = pl.multiple_of(g * SUB, SUB)
        there = pl.ds(pl.multiple_of((row0 + HALO) * SUB, SUB), SUB * SUB)

        def lane_block(j, carry):
            at = pl.multiple_of(j * STEP, STEP)
            coefs, values = [], []
            for p in range(parts):
                cols = pl.ds(pl.multiple_of(at + p * width, STEP), STEP)
                zone = zones[pl.ds(row0, SUB), cols]
                for f in range(per):
                    value = jnp.full(zone.shape, diff[f, 0], F32)
                    for z in range(1, diff.shape[1]):
                        value = jnp.where(zone == z, diff[f, z], value)
                    coefs.append(value)
                    values.append(fields[f, pl.ds(row0, SUB), cols])
            for buf, made in ((coef, coefs), (src, values)):
                turned = jnp.swapaxes(jnp.stack(made, 0), 0, 1)
                buf[there, pl.ds(at, STEP)] = turned.reshape(SUB * SUB, STEP)
            return carry

        lax.fori_loop(0, width // STEP, lane_block, 0)

    def prep_end(i, carry):
        prep(i * (groups - 1))
        return carry

    lax.fori_loop(0, 2, prep_end, 0)
    top = HALO * SUB
    for side, row in ((0, HALO), (1, rows)):
        halo_out[side] = jnp.concatenate(
            [src[row * SUB : row * SUB + top, :], coef[row * SUB : row * SUB + top, :]], 0
        ).astype(BF16)
    heard = (n - 1) + has_up.astype(jnp.int32) + has_down.astype(jnp.int32)
    pl.semaphore_wait(barrier, heard)

    def halo_copy(side):
        target = here - 1 if side == 0 else here + 1
        return pltpu.make_async_remote_copy(
            src_ref=halo_out.at[side],
            dst_ref=halo_in.at[1 - side],
            send_sem=halo_ssem.at[side],
            recv_sem=halo_rsem.at[1 - side],
            device_id={"space": target},
            device_id_type=MESH,
        )

    @pl.when(has_up)
    def _():
        halo_copy(0).start()

    @pl.when(has_down)
    def _():
        halo_copy(1).start()

    def prep_mid(g, carry):
        prep(g)
        return carry

    lax.fori_loop(1, groups - 1, prep_mid, 0)

    lane0 = iota2((SUB, 128), 1) == 0
    lane_last = iota2((SUB, 128), 1) == 127

    def from_east(x):
        rolled = pltpu.roll(x, width - 1, 1)
        tail = rolled[:, width - 128 :]
        tail = jnp.where(lane_last, pltpu.roll(tail, SUB - per, 0), tail)
        return jnp.concatenate([rolled[:, : width - 128], tail], 1)

    def from_west(x):
        rolled = pltpu.roll(x, 1, 1)
        head = rolled[:, :128]
        head = jnp.where(lane0, pltpu.roll(head, per, 0), head)
        return jnp.concatenate([head, rolled[:, 128:]], 1)

    def at_row(r):
        return pl.ds(pl.multiple_of(r * SUB, SUB), SUB)

    def first_row(r, carry):
        a, b, c = at_row(r - 1), at_row(r), at_row(r + 1)
        mine = coef[b, :]
        down = 0.5 * (mine + coef[c, :])
        up = 0.5 * (mine + coef[a, :])
        east = 0.5 * (mine + from_east(mine))
        west = from_west(east)
        outside = jnp.logical_or(
            jnp.logical_and(r < HALO, jnp.logical_not(has_up)),
            jnp.logical_and(r >= rows + HALO, jnp.logical_not(has_down)),
        )
        scale = jnp.where(outside, 0.0, 1.0).astype(F32)
        inv = scale / (1.0 + down + up + east + west)
        face_d[b, :] = down
        face_e[b, :] = east
        rdiag[b, :] = inv
        v = src[b, :]
        total = v + down * src[c, :] + up * src[a, :]
        total = total + east * from_east(v) + from_west(east * v)
        weight = RELAX_WEIGHTS[0]
        s1[b, :] = (1.0 - weight) * v + (weight * inv) * total
        return carry

    def later_row(old, new, weight, r, carry):
        a, b, c = at_row(r - 1), at_row(r), at_row(r + 1)
        v = old[b, :]
        east = face_e[b, :]
        total = src[b, :] + face_d[b, :] * old[c, :] + face_d[a, :] * old[a, :]
        total = total + east * from_east(v) + from_west(east * v)
        new[b, :] = (1.0 - weight) * v + (weight * rdiag[b, :]) * total
        return carry

    steps = (
        first_row,
        functools.partial(later_row, s1, s2, RELAX_WEIGHTS[1]),
        functools.partial(later_row, s2, s3, RELAX_WEIGHTS[2]),
    )
    done = [set() for _ in steps]

    def stencil(k):
        low, high = k * chunk_rows + HALO, (k + 1) * chunk_rows + HALO
        for number, step in enumerate(steps):
            grow = SWEEPS - 1 - number
            need = sorted(set(range(low - grow, high + grow)) - done[number])
            done[number].update(need)
            lax.fori_loop(need[0], need[-1] + 1, step, 0)
        for d in range(n):
            row = (low + 2 * d) * SUB
            sbuf[k, d] = s3[row : row + PAIR, :].astype(BF16)
        for c in sends(k):
            c.start()

    def all_copies(src_buf, dst_buf, k, send_sem, recv_sem, local_sem):
        copies = []
        for off in range(1, n):
            peer = lax.rem(me + off, n)
            copies.append(
                pltpu.make_async_remote_copy(
                    src_ref=src_buf.at[k, peer],
                    dst_ref=dst_buf.at[k, me],
                    send_sem=send_sem.at[k, off],
                    recv_sem=recv_sem.at[k, off],
                    device_id={"field": peer},
                    device_id_type=MESH,
                )
            )
        local = pltpu.make_async_copy(src_buf.at[k, me], dst_buf.at[k, me], local_sem.at[k])
        return copies + [local]

    def sends(k):
        return all_copies(sbuf, xbuf, k, ssem, rsem, lsem)

    def returns(k):
        return all_copies(rbuf, ret, k, rssem, rrsem, rlsem)

    def halo_wait():
        for slot, row, has in ((0, 0, has_up), (1, rows + HALO, has_down)):
            there = pl.ds(row * SUB, top)

            @pl.when(has)
            def _():
                copy = halo_copy(1 - slot)
                copy.wait_recv()
                both = halo_in[slot].astype(F32)
                src[there, :] = both[:top]
                coef[there, :] = both[top:]

            @pl.when(jnp.logical_not(has))
            def _():
                src[there, :] = jnp.zeros((top, width), F32)
                coef[there, :] = jnp.zeros((top, width), F32)

        @pl.when(has_up)
        def _():
            halo_copy(0).wait_send()

        @pl.when(has_down)
        def _():
            halo_copy(1).wait_send()

    def weights():
        depth = (n + 1) * PAIR
        bias = three_rows(0.5 * b_in[...])
        row, col = iota2((PAIR, depth), 0), iota2((PAIR, depth), 1)
        bias_cols = across(bias, (col == row + n * PAIR).astype(BF16))
        for v in range(variants):
            place = (row // per) * PAIR + v * per + lax.rem(row, per)
            pick = jnp.where(col == place, 0.5, 0.0).astype(BF16)
            spread = across(w_in[...], pick)
            w1[v * hid : (v + 1) * hid, :] = (spread + bias_cols).astype(BF16)
        square = (iota2((PAIR, PAIR), 0) == iota2((PAIR, PAIR), 1)).astype(BF16)
        w2[:, :hid] = w_mid[...] * jnp.asarray(0.5, BF16)
        w2[:, hid:] = across(three_rows(0.5 * b_mid[...]), square).astype(BF16)
        w3[:, :hid] = w_out[...]
        w3[:, hid:] = across(three_rows(b_out[...]), square).astype(BF16)
        rate_row[...] = jnp.zeros(rate_row.shape, F32)
        rate_row[0:1, 0 : FIELDS - 1] = rate[...].reshape(1, FIELDS - 1)
        ones = jnp.ones((PAIR, lanes_at_once), BF16)
        rate_col[...] = across(three_rows(rate_row[0:1, :])[:, :FIELDS], ones)
        for k in range(chunks):
            xbuf[k, n] = jnp.ones((PAIR, width), BF16)

    def surrogate(k):
        ones = jnp.ones((PAIR, lanes_at_once), BF16)
        for c in sends(k):
            c.wait()

        def block(j, carry):
            lanes = pl.ds(pl.multiple_of(j * lanes_at_once, lanes_at_once), lanes_at_once)
            x = xbuf[k, :, :, lanes].reshape((n + 1) * PAIR, lanes_at_once)
            heat_in = xbuf[k, n - 1, :, lanes].astype(F32)
            first, second, scaled = {}, {}, []

            def enter(v):
                first[v] = jnp.dot(w1[v * hid : (v + 1) * hid, :], x, preferred_element_type=F32)

            def middle(v):
                hidden = jnp.concatenate([halves_silu(first.pop(v)), ones], 0)
                second[v] = jnp.dot(w2[...], hidden, preferred_element_type=F32)

            def leave(v):
                hidden = jnp.concatenate([halves_silu(second.pop(v)), ones], 0)
                change = jnp.dot(w3[...], hidden, preferred_element_type=F32)
                last = v * per + per - 1
                heat = heat_in[last : last + 1] + change[FIELDS - 1 :]
                scaled.append(change * jnp.exp(rate_col[...] * jnp.tanh(heat)))

            enter(0)
            for v in range(variants):
                if v + 1 < variants:
                    enter(v + 1)
                middle(v)
                if v > 0:
                    leave(v - 1)
            leave(variants - 1)
            for s in range(n):
                block_out = jnp.concatenate([one[s * per : (s + 1) * per] for one in scaled], 0)
                rbuf[k, s, :, lanes] = block_out.astype(BF16)
            return carry

        lax.fori_loop(0, width // lanes_at_once, block, 0)
        for c in returns(k):
            c.start()

    def finish(k):
        for c in returns(k):
            c.wait()
        low = k * chunk_rows + HALO
        for d in range(n):
            row = (low + 2 * d) * SUB
            s3[row : row + PAIR, :] = s3[row : row + PAIR, :] + ret[k, d].astype(F32)
        for g in range(k * chunk_rows // SUB, (k + 1) * chunk_rows // SUB):

            def lane_block(j, carry, g=g):
                at = pl.multiple_of(j * STEP, STEP)
                slab = s3[(g * SUB + HALO) * SUB : ((g + 1) * SUB + HALO) * SUB, pl.ds(at, STEP)]
                turned = jnp.swapaxes(slab.reshape(SUB, SUB, STEP), 0, 1)
                for p in range(parts):
                    cols = pl.ds(pl.multiple_of(at + p * width, STEP), STEP)
                    for f in range(per):
                        out[f, pl.ds(g * SUB, SUB), cols] = turned[p * per + f]
                return carry

            lax.fori_loop(0, width // STEP, lane_block, 0)

    inner = list(range(1, chunks - 1))
    edge = [k for k in range(chunks) if k not in inner]
    for k in inner:
        stencil(k)
    weights()
    order = inner + edge
    begun = 0
    if inner:
        surrogate(order[0])
        begun = 1
    halo_wait()
    for k in edge:
        stencil(k)
    for i in range(begun, chunks):
        surrogate(order[i])
        if i > 0:
            finish(order[i - 1])
    finish(order[-1])


def on_device(
    n,
    n_space,
    fields,
    zone_ids,
    diffusivity,
    heat_rate,
    weight_in,
    bias_in,
    weight_mid,
    bias_mid,
    weight_out,
    bias_out,
):
    per, rows, columns = fields.shape
    width = columns * per // SUB
    variants = 2 * SUB // per
    lanes_at_once = block_lanes(width)
    hid = weight_mid.shape[0]
    chunks = rows // (2 * n)
    padded = (rows + 2 * HALO) * SUB
    vmem = pl.BlockSpec(memory_space=pltpu.VMEM)
    smem = pl.BlockSpec(memory_space=pltpu.SMEM)
    slab = pltpu.VMEM((padded, width), F32)
    dma = pltpu.SemaphoreType.DMA
    return pl.pallas_call(
        functools.partial(kernel, n, n_space),
        out_shape=jax.ShapeDtypeStruct(fields.shape, F32),
        in_specs=[vmem, vmem, smem] + [vmem] * 7,
        out_specs=vmem,
        scratch_shapes=[slab] * 8
        + [
            pltpu.VMEM((2, 2 * HALO * SUB, width), BF16),
            pltpu.VMEM((2, 2 * HALO * SUB, width), BF16),
            pltpu.VMEM((chunks, n, PAIR, width), BF16),
            pltpu.VMEM((chunks, n + 1, PAIR, width), BF16),
            pltpu.VMEM((chunks, n, PAIR, width), BF16),
            pltpu.VMEM((chunks, n, PAIR, width), BF16),
            pltpu.VMEM((variants * hid, (n + 1) * PAIR), BF16),
            pltpu.VMEM((hid, hid + PAIR), BF16),
            pltpu.VMEM((FIELDS, hid + PAIR), BF16),
            pltpu.VMEM((SUB, 128), F32),
            pltpu.VMEM((FIELDS, lanes_at_once), F32),
            dma((2,)),
            dma((2,)),
            dma((chunks, n)),
            dma((chunks, n)),
            dma((chunks, n)),
            dma((chunks, n)),
            dma((chunks,)),
            dma((chunks,)),
        ],
        compiler_params=pltpu.CompilerParams(
            collective_id=0, has_side_effects=True, vmem_limit_bytes=60 * 1024 * 1024
        ),
        cost_estimate=pl.CostEstimate(
            flops=2 * per * rows * columns // n * hid * (hid + 2 * FIELDS),
            bytes_accessed=9 * per * rows * columns,
            transcendentals=0,
        ),
    )(
        fields,
        zone_ids,
        diffusivity,
        heat_rate,
        weight_in.T,
        bias_in,
        weight_mid,
        bias_mid,
        weight_out,
        bias_out,
    )


def solution(mesh):
    n, n_space = mesh.shape["field"], mesh.shape["space"]
    return jax.shard_map(
        functools.partial(on_device, n, n_space),
        mesh=mesh,
        in_specs=(
            P("field", "space", None),
            P("space", None),
            P("field", None),
            P(),
            P(),
            P(),
            P(),
            P(),
            P(),
            P(),
        ),
        out_specs=P("field", "space", None),
        check_vma=False,
    )
```

```python
import functools

import jax
import jax.numpy as jnp
from jax import lax
from jax.experimental import pallas as pl
from jax.experimental.pallas import tpu as pltpu
from jax.sharding import PartitionSpec as P

FIELDS = 16
SWEEPS = 3
HALO = 3
SUB = 8
PAIR = 16
STEP = 256
RELAX_WEIGHTS = (0.8, 1.25, 0.95)
MESH = pl.DeviceIdType.MESH
F32 = jnp.float32
BF16 = jnp.bfloat16


def block_lanes(width):
    for once, step in ((512, 1024), (512, 512), (256, 768)):
        if width % step == 0:
            return once, step
    return 256, 256


def iota2(shape, axis):
    return lax.broadcasted_iota(jnp.int32, shape, axis)


def three_rows(row):
    row = row.reshape(1, -1)
    high = row.astype(BF16).astype(F32)
    rest = row - high
    mid = rest.astype(BF16).astype(F32)
    low = rest - mid
    index = iota2((PAIR, row.shape[1]), 0)
    zero = jnp.zeros((PAIR, row.shape[1]), F32)
    out = jnp.where(index == 0, high, zero)
    out = jnp.where(index == 1, mid, out)
    out = jnp.where(index == 2, low, out)
    return out.astype(BF16)


def across(rows16, select):
    return lax.dot_general(rows16, select, (((0,), (0,)), ((), ())), preferred_element_type=F32)


def halves_silu(pre):
    y = pre.astype(BF16)
    return y + y * jnp.tanh(y)


def kernel(
    n,
    n_space,
    fields,
    zones,
    diff,
    rate,
    w_in,
    b_in,
    w_mid,
    b_mid,
    w_out,
    b_out,
    out,
    src,
    coef,
    face_d,
    face_e,
    rdiag,
    s1,
    s2,
    s3,
    halo_out,
    halo_in,
    sbuf,
    xbuf,
    rbuf,
    ret,
    w1,
    w2,
    w3,
    rate_row,
    rate_col,
    halo_ssem,
    halo_rsem,
    ssem,
    rsem,
    rssem,
    rrsem,
    lsem,
    rlsem,
):
    per, rows, columns = fields.shape
    parts = SUB // per
    width = columns // parts
    variants = 2 * parts
    lanes_at_once, lanes_step = block_lanes(width)
    hid = w_mid.shape[0]
    chunks = rows // (2 * n)
    chunk_rows = rows // chunks
    groups = rows // SUB
    here = lax.axis_index("space")
    me = lax.axis_index("field")
    has_up = here > 0
    has_down = here < n_space - 1

    barrier = pltpu.get_barrier_semaphore()
    for off in range(1, n):
        pl.semaphore_signal(
            barrier, inc=1, device_id={"field": lax.rem(me + off, n)}, device_id_type=MESH
        )

    @pl.when(has_up)
    def _():
        pl.semaphore_signal(barrier, inc=1, device_id={"space": here - 1}, device_id_type=MESH)

    @pl.when(has_down)
    def _():
        pl.semaphore_signal(barrier, inc=1, device_id={"space": here + 1}, device_id_type=MESH)

    def prep(g):
        row0 = pl.multiple_of(g * SUB, SUB)
        there = pl.ds(pl.multiple_of((row0 + HALO) * SUB, SUB), SUB * SUB)

        def lane_block(j, carry):
            at = pl.multiple_of(j * STEP, STEP)
            coefs, values = [], []
            for p in range(parts):
                cols = pl.ds(pl.multiple_of(at + p * width, STEP), STEP)
                zone = zones[pl.ds(row0, SUB), cols]
                for f in range(per):
                    value = jnp.full(zone.shape, diff[f, 0], F32)
                    for z in range(1, diff.shape[1]):
                        value = jnp.where(zone == z, diff[f, z], value)
                    coefs.append(value)
                    values.append(fields[f, pl.ds(row0, SUB), cols])
            for buf, made in ((coef, coefs), (src, values)):
                turned = jnp.swapaxes(jnp.stack(made, 0), 0, 1)
                buf[there, pl.ds(at, STEP)] = turned.reshape(SUB * SUB, STEP)
            return carry

        lax.fori_loop(0, width // STEP, lane_block, 0)

    def prep_end(i, carry):
        prep(i * (groups - 1))
        return carry

    lax.fori_loop(0, 2, prep_end, 0)
    top = HALO * SUB
    for side, row in ((0, HALO), (1, rows)):
        halo_out[side] = jnp.concatenate(
            [src[row * SUB : row * SUB + top, :], coef[row * SUB : row * SUB + top, :]], 0
        ).astype(BF16)
    heard = (n - 1) + has_up.astype(jnp.int32) + has_down.astype(jnp.int32)
    pl.semaphore_wait(barrier, heard)

    def halo_copy(side):
        target = here - 1 if side == 0 else here + 1
        return pltpu.make_async_remote_copy(
            src_ref=halo_out.at[side],
            dst_ref=halo_in.at[1 - side],
            send_sem=halo_ssem.at[side],
            recv_sem=halo_rsem.at[1 - side],
            device_id={"space": target},
            device_id_type=MESH,
        )

    @pl.when(has_up)
    def _():
        halo_copy(0).start()

    @pl.when(has_down)
    def _():
        halo_copy(1).start()

    def prep_mid(g, carry):
        prep(g)
        return carry

    lax.fori_loop(1, groups - 1, prep_mid, 0)

    lane0 = iota2((SUB, 128), 1) == 0
    lane_last = iota2((SUB, 128), 1) == 127

    def from_east(x):
        rolled = pltpu.roll(x, width - 1, 1)
        tail = rolled[:, width - 128 :]
        tail = jnp.where(lane_last, pltpu.roll(tail, SUB - per, 0), tail)
        return jnp.concatenate([rolled[:, : width - 128], tail], 1)

    def from_west(x):
        rolled = pltpu.roll(x, 1, 1)
        head = rolled[:, :128]
        head = jnp.where(lane0, pltpu.roll(head, per, 0), head)
        return jnp.concatenate([head, rolled[:, 128:]], 1)

    def at_row(r):
        return pl.ds(pl.multiple_of(r * SUB, SUB), SUB)

    def first_row(r, carry):
        a, b, c = at_row(r - 1), at_row(r), at_row(r + 1)
        mine = coef[b, :]
        down = 0.5 * (mine + coef[c, :])
        up = 0.5 * (mine + coef[a, :])
        east = 0.5 * (mine + from_east(mine))
        west = from_west(east)
        outside = jnp.logical_or(
            jnp.logical_and(r < HALO, jnp.logical_not(has_up)),
            jnp.logical_and(r >= rows + HALO, jnp.logical_not(has_down)),
        )
        scale = jnp.where(outside, 0.0, 1.0).astype(F32)
        inv = scale / (1.0 + down + up + east + west)
        face_d[b, :] = down
        face_e[b, :] = east
        rdiag[b, :] = inv
        v = src[b, :]
        total = v + down * src[c, :] + up * src[a, :]
        total = total + east * from_east(v) + from_west(east * v)
        weight = RELAX_WEIGHTS[0]
        s1[b, :] = (1.0 - weight) * v + (weight * inv) * total
        return carry

    def later_row(old, new, weight, r, carry):
        a, b, c = at_row(r - 1), at_row(r), at_row(r + 1)
        v = old[b, :]
        east = face_e[b, :]
        total = src[b, :] + face_d[b, :] * old[c, :] + face_d[a, :] * old[a, :]
        total = total + east * from_east(v) + from_west(east * v)
        new[b, :] = (1.0 - weight) * v + (weight * rdiag[b, :]) * total
        return carry

    steps = (
        first_row,
        functools.partial(later_row, s1, s2, RELAX_WEIGHTS[1]),
        functools.partial(later_row, s2, s3, RELAX_WEIGHTS[2]),
    )
    done = [set() for _ in steps]

    def stencil(k):
        low, high = k * chunk_rows + HALO, (k + 1) * chunk_rows + HALO
        for number, step in enumerate(steps):
            grow = SWEEPS - 1 - number
            need = sorted(set(range(low - grow, high + grow)) - done[number])
            done[number].update(need)
            lax.fori_loop(need[0], need[-1] + 1, step, 0)
        for d in range(n):
            row = (low + 2 * d) * SUB
            sbuf[k, d] = s3[row : row + PAIR, :].astype(BF16)
        for c in sends(k):
            c.start()

    def all_copies(src_buf, dst_buf, k, send_sem, recv_sem, local_sem, cols=slice(None)):
        copies = []
        for off in range(1, n):
            peer = lax.rem(me + off, n)
            copies.append(
                pltpu.make_async_remote_copy(
                    src_ref=src_buf.at[k, peer, :, cols],
                    dst_ref=dst_buf.at[k, me, :, cols],
                    send_sem=send_sem.at[k, off],
                    recv_sem=recv_sem.at[k, off],
                    device_id={"field": peer},
                    device_id_type=MESH,
                )
            )
        local = pltpu.make_async_copy(
            src_buf.at[k, me, :, cols], dst_buf.at[k, me, :, cols], local_sem.at[k]
        )
        return copies + [local]

    def sends(k):
        return all_copies(sbuf, xbuf, k, ssem, rsem, lsem)

    def returns(k, cols=slice(None)):
        return all_copies(rbuf, ret, k, rssem, rrsem, rlsem, cols)

    def halo_wait():
        for slot, row, has in ((0, 0, has_up), (1, rows + HALO, has_down)):
            there = pl.ds(row * SUB, top)

            @pl.when(has)
            def _():
                copy = halo_copy(1 - slot)
                copy.wait_recv()
                both = halo_in[slot].astype(F32)
                src[there, :] = both[:top]
                coef[there, :] = both[top:]

            @pl.when(jnp.logical_not(has))
            def _():
                src[there, :] = jnp.zeros((top, width), F32)
                coef[there, :] = jnp.zeros((top, width), F32)

        @pl.when(has_up)
        def _():
            halo_copy(0).wait_send()

        @pl.when(has_down)
        def _():
            halo_copy(1).wait_send()

    def weights():
        depth = (n + 1) * PAIR
        bias = three_rows(0.5 * b_in[...])
        row, col = iota2((PAIR, depth), 0), iota2((PAIR, depth), 1)
        bias_cols = across(bias, (col == row + n * PAIR).astype(BF16))
        for v in range(variants):
            place = (row // per) * PAIR + v * per + lax.rem(row, per)
            pick = jnp.where(col == place, 0.5, 0.0).astype(BF16)
            spread = across(w_in[...], pick)
            w1[v * hid : (v + 1) * hid, :] = (spread + bias_cols).astype(BF16)
        square = (iota2((PAIR, PAIR), 0) == iota2((PAIR, PAIR), 1)).astype(BF16)
        w2[:, :hid] = w_mid[...] * jnp.asarray(0.5, BF16)
        w2[:, hid:] = across(three_rows(0.5 * b_mid[...]), square).astype(BF16)
        w3[:, :hid] = w_out[...]
        w3[:, hid:] = across(three_rows(b_out[...]), square).astype(BF16)
        rate_row[...] = jnp.zeros(rate_row.shape, F32)
        rate_row[0:1, 0 : FIELDS - 1] = rate[...].reshape(1, FIELDS - 1)
        ones = jnp.ones((PAIR, lanes_at_once), BF16)
        rate_col[...] = across(three_rows(rate_row[0:1, :])[:, :FIELDS], ones)
        for k in range(chunks):
            xbuf[k, n] = jnp.ones((PAIR, width), BF16)

    def surrogate(k):
        ones = jnp.ones((PAIR, lanes_at_once), BF16)
        for c in sends(k):
            c.wait()

        def block(j, carry):
            start = pl.multiple_of(j * lanes_step, lanes_step)
            subs = lanes_step // lanes_at_once
            units = [(sub, v) for sub in range(subs) for v in range(variants)]
            lanes = [
                pl.ds(pl.multiple_of(start + sub * lanes_at_once, lanes_at_once), lanes_at_once)
                for sub in range(subs)
            ]
            x = [xbuf[k, :, :, at].reshape((n + 1) * PAIR, lanes_at_once) for at in lanes]
            heat_in = [xbuf[k, n - 1, :, at].astype(F32) for at in lanes]
            first, second, scaled = {}, {}, []

            def enter(u):
                sub, v = units[u]
                rows_v = w1[v * hid : (v + 1) * hid, :]
                first[u] = jnp.dot(rows_v, x[sub], preferred_element_type=F32)

            def middle(u):
                hidden = jnp.concatenate([halves_silu(first.pop(u)), ones], 0)
                second[u] = jnp.dot(w2[...], hidden, preferred_element_type=F32)

            def leave(u):
                sub, v = units[u]
                hidden = jnp.concatenate([halves_silu(second.pop(u)), ones], 0)
                change = jnp.dot(w3[...], hidden, preferred_element_type=F32)
                last = v * per + per - 1
                heat = heat_in[sub][last : last + 1] + change[FIELDS - 1 :]
                scaled.append(change * jnp.exp(rate_col[...] * jnp.tanh(heat)))
                if v == variants - 1:
                    for s in range(n):
                        pieces = [one[s * per : (s + 1) * per] for one in scaled]
                        rbuf[k, s, :, lanes[sub]] = jnp.concatenate(pieces, 0).astype(BF16)
                    scaled.clear()

            enter(0)
            for u in range(len(units)):
                if u + 1 < len(units):
                    enter(u + 1)
                middle(u)
                if u > 0:
                    leave(u - 1)
            leave(len(units) - 1)
            for c in returns(k, pl.ds(start, lanes_step)):
                c.start()
            return carry

        lax.fori_loop(0, width // lanes_step, block, 0)

    def finish(k):
        for c in returns(k):
            c.wait()
        low = k * chunk_rows + HALO
        for d in range(n):
            row = (low + 2 * d) * SUB
            s3[row : row + PAIR, :] = s3[row : row + PAIR, :] + ret[k, d].astype(F32)
        for g in range(k * chunk_rows // SUB, (k + 1) * chunk_rows // SUB):

            def lane_block(j, carry, g=g):
                at = pl.multiple_of(j * STEP, STEP)
                slab = s3[(g * SUB + HALO) * SUB : ((g + 1) * SUB + HALO) * SUB, pl.ds(at, STEP)]
                turned = jnp.swapaxes(slab.reshape(SUB, SUB, STEP), 0, 1)
                for p in range(parts):
                    cols = pl.ds(pl.multiple_of(at + p * width, STEP), STEP)
                    for f in range(per):
                        out[f, pl.ds(g * SUB, SUB), cols] = turned[p * per + f]
                return carry

            lax.fori_loop(0, width // STEP, lane_block, 0)

    inner = list(range(1, chunks - 1))
    edge = [k for k in range(chunks) if k not in inner]
    for k in inner:
        stencil(k)
    weights()
    order = inner + edge
    begun = 0
    if inner:
        surrogate(order[0])
        begun = 1
    halo_wait()
    for k in edge:
        stencil(k)
    for i in range(begun, chunks):
        surrogate(order[i])
        if i > 0:
            finish(order[i - 1])
    finish(order[-1])


def on_device(
    n,
    n_space,
    fields,
    zone_ids,
    diffusivity,
    heat_rate,
    weight_in,
    bias_in,
    weight_mid,
    bias_mid,
    weight_out,
    bias_out,
):
    per, rows, columns = fields.shape
    width = columns * per // SUB
    variants = 2 * SUB // per
    lanes_at_once, lanes_step = block_lanes(width)
    hid = weight_mid.shape[0]
    chunks = rows // (2 * n)
    padded = (rows + 2 * HALO) * SUB
    vmem = pl.BlockSpec(memory_space=pltpu.VMEM)
    smem = pl.BlockSpec(memory_space=pltpu.SMEM)
    slab = pltpu.VMEM((padded, width), F32)
    dma = pltpu.SemaphoreType.DMA
    return pl.pallas_call(
        functools.partial(kernel, n, n_space),
        out_shape=jax.ShapeDtypeStruct(fields.shape, F32),
        in_specs=[vmem, vmem, smem] + [vmem] * 7,
        out_specs=vmem,
        scratch_shapes=[slab] * 8
        + [
            pltpu.VMEM((2, 2 * HALO * SUB, width), BF16),
            pltpu.VMEM((2, 2 * HALO * SUB, width), BF16),
            pltpu.VMEM((chunks, n, PAIR, width), BF16),
            pltpu.VMEM((chunks, n + 1, PAIR, width), BF16),
            pltpu.VMEM((chunks, n, PAIR, width), BF16),
            pltpu.VMEM((chunks, n, PAIR, width), BF16),
            pltpu.VMEM((variants * hid, (n + 1) * PAIR), BF16),
            pltpu.VMEM((hid, hid + PAIR), BF16),
            pltpu.VMEM((FIELDS, hid + PAIR), BF16),
            pltpu.VMEM((SUB, 128), F32),
            pltpu.VMEM((FIELDS, lanes_at_once), F32),
            dma((2,)),
            dma((2,)),
            dma((chunks, n)),
            dma((chunks, n)),
            dma((chunks, n)),
            dma((chunks, n)),
            dma((chunks,)),
            dma((chunks,)),
        ],
        compiler_params=pltpu.CompilerParams(
            collective_id=0, has_side_effects=True, vmem_limit_bytes=60 * 1024 * 1024
        ),
        cost_estimate=pl.CostEstimate(
            flops=2 * per * rows * columns // n * hid * (hid + 2 * FIELDS),
            bytes_accessed=9 * per * rows * columns,
            transcendentals=0,
        ),
    )(
        fields,
        zone_ids,
        diffusivity,
        heat_rate,
        weight_in.T,
        bias_in,
        weight_mid,
        bias_mid,
        weight_out,
        bias_out,
    )


def solution(mesh):
    n, n_space = mesh.shape["field"], mesh.shape["space"]
    return jax.shard_map(
        functools.partial(on_device, n, n_space),
        mesh=mesh,
        in_specs=(
            P("field", "space", None),
            P("space", None),
            P("field", None),
            P(),
            P(),
            P(),
            P(),
            P(),
            P(),
            P(),
        ),
        out_specs=P("field", "space", None),
        check_vma=False,
    )
```

```python
import functools

import jax
import jax.numpy as jnp
from jax import lax
from jax.experimental import pallas as pl
from jax.experimental.pallas import tpu as pltpu
from jax.sharding import PartitionSpec as P

FIELDS = 16
SWEEPS = 3
HALO = 3
SUB = 8
PAIR = 16
STEP = 256
RELAX_WEIGHTS = (0.8, 1.25, 0.95)
MESH = pl.DeviceIdType.MESH
F32 = jnp.float32
BF16 = jnp.bfloat16


def block_lanes(width):
    for once, step in ((512, 1024), (512, 512), (256, 768)):
        if width % step == 0:
            return once, step
    return 256, 256


def iota2(shape, axis):
    return lax.broadcasted_iota(jnp.int32, shape, axis)


def three_rows(row):
    row = row.reshape(1, -1)
    high = row.astype(BF16).astype(F32)
    rest = row - high
    mid = rest.astype(BF16).astype(F32)
    low = rest - mid
    index = iota2((PAIR, row.shape[1]), 0)
    zero = jnp.zeros((PAIR, row.shape[1]), F32)
    out = jnp.where(index == 0, high, zero)
    out = jnp.where(index == 1, mid, out)
    out = jnp.where(index == 2, low, out)
    return out.astype(BF16)


def across(rows16, select):
    return lax.dot_general(rows16, select, (((0,), (0,)), ((), ())), preferred_element_type=F32)


def halves_silu(pre):
    y = pre.astype(BF16)
    return y + y * jnp.tanh(y)


def kernel(
    n,
    n_space,
    fields,
    zones,
    diff,
    rate,
    w_in,
    b_in,
    w_mid,
    b_mid,
    w_out,
    b_out,
    out,
    states,
    coef,
    face_d,
    face_e,
    rdiag,
    halo_out,
    halo_in,
    sbuf,
    xbuf,
    rbuf,
    ret,
    w1,
    w2,
    w3,
    rate_row,
    rate_col,
    halo_ssem,
    halo_rsem,
    ssem,
    rsem,
    rssem,
    rrsem,
    lsem,
    rlsem,
):
    per, rows, columns = fields.shape
    src, s3 = states.at[0], states.at[SWEEPS]
    parts = SUB // per
    width = columns // parts
    variants = 2 * parts
    lanes_at_once, lanes_step = block_lanes(width)
    hid = w_mid.shape[0]
    chunks = rows // (2 * n)
    chunk_rows = rows // chunks
    groups = rows // SUB
    here = lax.axis_index("space")
    me = lax.axis_index("field")
    has_up = here > 0
    has_down = here < n_space - 1

    barrier = pltpu.get_barrier_semaphore()
    for off in range(1, n):
        pl.semaphore_signal(
            barrier, inc=1, device_id={"field": lax.rem(me + off, n)}, device_id_type=MESH
        )

    @pl.when(has_up)
    def _():
        pl.semaphore_signal(barrier, inc=1, device_id={"space": here - 1}, device_id_type=MESH)

    @pl.when(has_down)
    def _():
        pl.semaphore_signal(barrier, inc=1, device_id={"space": here + 1}, device_id_type=MESH)

    def prep(g):
        row0 = pl.multiple_of(g * SUB, SUB)
        there = pl.ds(pl.multiple_of((row0 + HALO) * SUB, SUB), SUB * SUB)

        def lane_block(j, carry):
            at = pl.multiple_of(j * STEP, STEP)
            coefs, values = [], []
            for p in range(parts):
                cols = pl.ds(pl.multiple_of(at + p * width, STEP), STEP)
                zone = zones[pl.ds(row0, SUB), cols]
                for f in range(per):
                    value = jnp.full(zone.shape, diff[f, 0], F32)
                    for z in range(1, diff.shape[1]):
                        value = jnp.where(zone == z, diff[f, z], value)
                    coefs.append(value)
                    values.append(fields[f, pl.ds(row0, SUB), cols])
            for buf, made in ((coef, coefs), (src, values)):
                turned = jnp.swapaxes(jnp.stack(made, 0), 0, 1)
                buf[there, pl.ds(at, STEP)] = turned.reshape(SUB * SUB, STEP)
            return carry

        lax.fori_loop(0, width // STEP, lane_block, 0)

    def prep_end(i, carry):
        prep(i * (groups - 1))
        return carry

    lax.fori_loop(0, 2, prep_end, 0)
    top = HALO * SUB
    for side, row in ((0, HALO), (1, rows)):
        halo_out[side] = jnp.concatenate(
            [src[row * SUB : row * SUB + top, :], coef[row * SUB : row * SUB + top, :]], 0
        ).astype(BF16)
    heard = (n - 1) + has_up.astype(jnp.int32) + has_down.astype(jnp.int32)
    pl.semaphore_wait(barrier, heard)

    def halo_copy(side):
        target = here - 1 if side == 0 else here + 1
        return pltpu.make_async_remote_copy(
            src_ref=halo_out.at[side],
            dst_ref=halo_in.at[1 - side],
            send_sem=halo_ssem.at[side],
            recv_sem=halo_rsem.at[1 - side],
            device_id={"space": target},
            device_id_type=MESH,
        )

    @pl.when(has_up)
    def _():
        halo_copy(0).start()

    @pl.when(has_down)
    def _():
        halo_copy(1).start()

    def prep_mid(g, carry):
        prep(g)
        return carry

    lax.fori_loop(1, groups - 1, prep_mid, 0)

    lane0 = iota2((SUB, 128), 1) == 0
    lane_last = iota2((SUB, 128), 1) == 127

    def from_east(x):
        rolled = pltpu.roll(x, width - 1, 1)
        tail = rolled[:, width - 128 :]
        tail = jnp.where(lane_last, pltpu.roll(tail, SUB - per, 0), tail)
        return jnp.concatenate([rolled[:, : width - 128], tail], 1)

    def from_west(x):
        rolled = pltpu.roll(x, 1, 1)
        head = rolled[:, :128]
        head = jnp.where(lane0, pltpu.roll(head, per, 0), head)
        return jnp.concatenate([head, rolled[:, 128:]], 1)

    def at_row(r):
        return pl.ds(pl.multiple_of(r * SUB, SUB), SUB)

    def face_row(r, carry):
        a, b, c = at_row(r - 1), at_row(r), at_row(r + 1)
        mine = coef[b, :]
        down = 0.5 * (mine + coef[c, :])
        up = 0.5 * (mine + coef[a, :])
        east = 0.5 * (mine + from_east(mine))
        west = from_west(east)
        outside = jnp.logical_or(
            jnp.logical_and(r < HALO, jnp.logical_not(has_up)),
            jnp.logical_and(r >= rows + HALO, jnp.logical_not(has_down)),
        )
        scale = jnp.where(outside, 0.0, 1.0).astype(F32)
        face_d[b, :] = down
        face_e[b, :] = east
        rdiag[b, :] = scale / (1.0 + down + up + east + west)
        return carry

    def sweep_row(sweep, weight, r, carry):
        a, b, c = at_row(r - 1), at_row(r), at_row(r + 1)
        v = states[sweep, b, :]
        east = face_e[b, :]
        total = src[b, :] + face_d[b, :] * states[sweep, c, :] + face_d[a, :] * states[sweep, a, :]
        total = total + east * from_east(v) + from_west(east * v)
        states[sweep + 1, b, :] = (1.0 - weight) * v + (weight * rdiag[b, :]) * total
        return carry

    done = [set() for _ in range(SWEEPS)]
    faced = set()

    def faces(need):
        need = sorted(set(need) - faced)
        faced.update(need)
        for start in [r for r in need if r - 1 not in need]:
            stop = start
            while stop in need:
                stop += 1
            lax.fori_loop(start, stop, face_row, 0)

    def bounds(k):
        return k * chunk_rows + HALO, (k + 1) * chunk_rows + HALO

    def sweep_rows(k, sweep):
        low, high = bounds(k)
        grow = SWEEPS - 1 - sweep
        need = sorted(set(range(low - grow, high + grow)) - done[sweep])
        done[sweep].update(need)
        return need

    def stencil(k):
        low, high = bounds(k)
        lowest = max(low - SWEEPS, 0)
        faces(range(lowest if lowest > 0 else 1, min(high + SWEEPS, rows + 2 * HALO - 1)))
        for sweep in range(SWEEPS):
            need = sweep_rows(k, sweep)
            step = functools.partial(sweep_row, sweep, RELAX_WEIGHTS[sweep])
            lax.fori_loop(need[0], need[-1] + 1, step, 0)
        send(k)

    def send(k):
        low = bounds(k)[0]
        for d in range(n):
            row = (low + 2 * d) * SUB
            sbuf[k, d] = s3[row : row + PAIR, :].astype(BF16)
        for c in sends(k):
            c.start()

    def all_copies(src_buf, dst_buf, k, send_sem, recv_sem, local_sem, cols=slice(None)):
        copies = []
        for off in range(1, n):
            peer = lax.rem(me + off, n)
            copies.append(
                pltpu.make_async_remote_copy(
                    src_ref=src_buf.at[k, peer, :, cols],
                    dst_ref=dst_buf.at[k, me, :, cols],
                    send_sem=send_sem.at[k, off],
                    recv_sem=recv_sem.at[k, off],
                    device_id={"field": peer},
                    device_id_type=MESH,
                )
            )
        local = pltpu.make_async_copy(
            src_buf.at[k, me, :, cols], dst_buf.at[k, me, :, cols], local_sem.at[k]
        )
        return copies + [local]

    def sends(k):
        return all_copies(sbuf, xbuf, k, ssem, rsem, lsem)

    def returns(k, cols=slice(None)):
        return all_copies(rbuf, ret, k, rssem, rrsem, rlsem, cols)

    def halo_wait():
        for slot, row, has in ((0, 0, has_up), (1, rows + HALO, has_down)):
            there = pl.ds(row * SUB, top)

            @pl.when(has)
            def _():
                copy = halo_copy(1 - slot)
                copy.wait_recv()
                both = halo_in[slot].astype(F32)
                src[there, :] = both[:top]
                coef[there, :] = both[top:]

            @pl.when(jnp.logical_not(has))
            def _():
                src[there, :] = jnp.zeros((top, width), F32)
                coef[there, :] = jnp.zeros((top, width), F32)

        @pl.when(has_up)
        def _():
            halo_copy(0).wait_send()

        @pl.when(has_down)
        def _():
            halo_copy(1).wait_send()

        face_d[0:SUB, :] = 0.5 * (coef[0:SUB, :] + coef[SUB : 2 * SUB, :])

    def weights():
        depth = (n + 1) * PAIR
        bias = three_rows(0.5 * b_in[...])
        row, col = iota2((PAIR, depth), 0), iota2((PAIR, depth), 1)
        bias_cols = across(bias, (col == row + n * PAIR).astype(BF16))
        for v in range(variants):
            place = (row // per) * PAIR + v * per + lax.rem(row, per)
            pick = jnp.where(col == place, 0.5, 0.0).astype(BF16)
            spread = across(w_in[...], pick)
            w1[v * hid : (v + 1) * hid, :] = (spread + bias_cols).astype(BF16)
        square = (iota2((PAIR, PAIR), 0) == iota2((PAIR, PAIR), 1)).astype(BF16)
        w2[:, :hid] = w_mid[...] * jnp.asarray(0.5, BF16)
        w2[:, hid:] = across(three_rows(0.5 * b_mid[...]), square).astype(BF16)
        w3[:, :hid] = w_out[...]
        w3[:, hid:] = across(three_rows(b_out[...]), square).astype(BF16)
        rate_row[...] = jnp.zeros(rate_row.shape, F32)
        rate_row[0:1, 0 : FIELDS - 1] = rate[...].reshape(1, FIELDS - 1)
        ones = jnp.ones((PAIR, lanes_at_once), BF16)
        rate_col[...] = across(three_rows(rate_row[0:1, :])[:, :FIELDS], ones)
        for k in range(chunks):
            xbuf[k, n] = jnp.ones((PAIR, width), BF16)

    def surrogate(k, beside=None):
        ones = jnp.ones((PAIR, lanes_at_once), BF16)
        for c in sends(k):
            c.wait()

        def block(j, carry):
            start = pl.multiple_of(j * lanes_step, lanes_step)
            subs = lanes_step // lanes_at_once
            units = [(sub, v) for sub in range(subs) for v in range(variants)]
            lanes = [
                pl.ds(pl.multiple_of(start + sub * lanes_at_once, lanes_at_once), lanes_at_once)
                for sub in range(subs)
            ]
            x = [xbuf[k, :, :, at].reshape((n + 1) * PAIR, lanes_at_once) for at in lanes]
            heat_in = [xbuf[k, n - 1, :, at].astype(F32) for at in lanes]
            first, second, scaled = {}, {}, []

            def enter(sub):
                every = jnp.dot(w1[...], x[sub], preferred_element_type=F32)
                for v in range(variants):
                    first[sub * variants + v] = every[v * hid : (v + 1) * hid]

            def middle(u):
                hidden = jnp.concatenate([halves_silu(first.pop(u)), ones], 0)
                second[u] = jnp.dot(w2[...], hidden, preferred_element_type=F32)

            def leave(u):
                sub, v = units[u]
                hidden = jnp.concatenate([halves_silu(second.pop(u)), ones], 0)
                change = jnp.dot(w3[...], hidden, preferred_element_type=F32)
                last = v * per + per - 1
                heat = heat_in[sub][last : last + 1] + change[FIELDS - 1 :]
                scaled.append(change * jnp.exp(rate_col[...] * jnp.tanh(heat)))
                if v == variants - 1:
                    for s in range(n):
                        pieces = [one[s * per : (s + 1) * per] for one in scaled]
                        rbuf[k, s, :, lanes[sub]] = jnp.concatenate(pieces, 0).astype(BF16)
                    scaled.clear()

            enter(0)
            for u in range(len(units)):
                if units[u][1] == variants // 2 and units[u][0] + 1 < subs:
                    enter(units[u][0] + 1)
                middle(u)
                if beside is not None:
                    beside(j, u)
                if u > 0:
                    leave(u - 1)
            leave(len(units) - 1)
            for c in returns(k, pl.ds(start, lanes_step)):
                c.start()
            return carry

        lax.fori_loop(0, width // lanes_step, block, 0)

    def finish(k):
        for c in returns(k):
            c.wait()
        low = k * chunk_rows + HALO
        for d in range(n):
            row = (low + 2 * d) * SUB
            s3[row : row + PAIR, :] = s3[row : row + PAIR, :] + ret[k, d].astype(F32)
        for g in range(k * chunk_rows // SUB, (k + 1) * chunk_rows // SUB):

            def lane_block(j, carry, g=g):
                at = pl.multiple_of(j * STEP, STEP)
                slab = s3[(g * SUB + HALO) * SUB : ((g + 1) * SUB + HALO) * SUB, pl.ds(at, STEP)]
                turned = jnp.swapaxes(slab.reshape(SUB, SUB, STEP), 0, 1)
                for p in range(parts):
                    cols = pl.ds(pl.multiple_of(at + p * width, STEP), STEP)
                    for f in range(per):
                        out[f, pl.ds(g * SUB, SUB), cols] = turned[p * per + f]
                return carry

            lax.fori_loop(0, width // STEP, lane_block, 0)

    inner = list(range(1, chunks - 1))
    edge = [k for k in range(chunks) if k not in inner]
    order = inner + edge
    units = lanes_step // lanes_at_once * variants
    hosted = len(inner) == 2 and width // lanes_step == SWEEPS and chunk_rows == units
    for k in inner:
        stencil(k)
    weights()
    halo_wait()
    if not hosted:
        for k in edge:
            stencil(k)
        for i, k in enumerate(order):
            surrogate(k)
            if i > 0:
                finish(order[i - 1])
        finish(order[-1])
        return

    for k in edge:
        low, high = bounds(k)
        faces(range(max(low - 2, 1), min(high + 2, rows + 2 * HALO - 1)))

    def beside(k):
        starts = [sweep_rows(k, sweep) for sweep in range(SWEEPS)]
        stride = starts[1][0] - starts[0][0]
        start = starts[0][0]

        def row(j, u):
            weight = jnp.where(j == 0, RELAX_WEIGHTS[0], RELAX_WEIGHTS[1])
            weight = jnp.where(j == 2, RELAX_WEIGHTS[2], weight).astype(F32)
            sweep_row(j, weight, start + stride * j + u, 0)

        return row

    for i, k in enumerate(order):
        surrogate(k, beside(edge[i]) if i < len(edge) else None)
        if i < len(edge):
            send(edge[i])
        if i > 0:
            finish(order[i - 1])
    finish(order[-1])


def on_device(
    n,
    n_space,
    fields,
    zone_ids,
    diffusivity,
    heat_rate,
    weight_in,
    bias_in,
    weight_mid,
    bias_mid,
    weight_out,
    bias_out,
):
    per, rows, columns = fields.shape
    width = columns * per // SUB
    variants = 2 * SUB // per
    lanes_at_once, lanes_step = block_lanes(width)
    hid = weight_mid.shape[0]
    chunks = rows // (2 * n)
    padded = (rows + 2 * HALO) * SUB
    vmem = pl.BlockSpec(memory_space=pltpu.VMEM)
    smem = pl.BlockSpec(memory_space=pltpu.SMEM)
    slab = pltpu.VMEM((padded, width), F32)
    dma = pltpu.SemaphoreType.DMA
    return pl.pallas_call(
        functools.partial(kernel, n, n_space),
        out_shape=jax.ShapeDtypeStruct(fields.shape, F32),
        in_specs=[vmem, vmem, smem] + [vmem] * 7,
        out_specs=vmem,
        scratch_shapes=[pltpu.VMEM((SWEEPS + 1, padded, width), F32)]
        + [slab] * 4
        + [
            pltpu.VMEM((2, 2 * HALO * SUB, width), BF16),
            pltpu.VMEM((2, 2 * HALO * SUB, width), BF16),
            pltpu.VMEM((chunks, n, PAIR, width), BF16),
            pltpu.VMEM((chunks, n + 1, PAIR, width), BF16),
            pltpu.VMEM((chunks, n, PAIR, width), BF16),
            pltpu.VMEM((chunks, n, PAIR, width), BF16),
            pltpu.VMEM((variants * hid, (n + 1) * PAIR), BF16),
            pltpu.VMEM((hid, hid + PAIR), BF16),
            pltpu.VMEM((FIELDS, hid + PAIR), BF16),
            pltpu.VMEM((SUB, 128), F32),
            pltpu.VMEM((FIELDS, lanes_at_once), F32),
            dma((2,)),
            dma((2,)),
            dma((chunks, n)),
            dma((chunks, n)),
            dma((chunks, n)),
            dma((chunks, n)),
            dma((chunks,)),
            dma((chunks,)),
        ],
        compiler_params=pltpu.CompilerParams(
            collective_id=0, has_side_effects=True, vmem_limit_bytes=60 * 1024 * 1024
        ),
        cost_estimate=pl.CostEstimate(
            flops=2 * per * rows * columns // n * hid * (hid + 2 * FIELDS),
            bytes_accessed=9 * per * rows * columns,
            transcendentals=0,
        ),
    )(
        fields,
        zone_ids,
        diffusivity,
        heat_rate,
        weight_in.T,
        bias_in,
        weight_mid,
        bias_mid,
        weight_out,
        bias_out,
    )


def solution(mesh):
    n, n_space = mesh.shape["field"], mesh.shape["space"]
    return jax.shard_map(
        functools.partial(on_device, n, n_space),
        mesh=mesh,
        in_specs=(
            P("field", "space", None),
            P("space", None),
            P("field", None),
            P(),
            P(),
            P(),
            P(),
            P(),
            P(),
            P(),
        ),
        out_specs=P("field", "space", None),
        check_vma=False,
    )
```

```python
import functools

import jax
import jax.numpy as jnp
from jax import lax
from jax.experimental import pallas as pl
from jax.experimental.pallas import tpu as pltpu
from jax.sharding import PartitionSpec as P

FIELDS = 16
SWEEPS = 3
HALO = 3
SUB = 8
PAIR = 16
STEP = 256
RELAX_WEIGHTS = (0.8, 1.25, 0.95)
MESH = pl.DeviceIdType.MESH
F32 = jnp.float32
BF16 = jnp.bfloat16


def block_lanes(width):
    for once, step in ((512, 1024), (512, 512), (256, 768)):
        if width % step == 0:
            return once, step
    return 256, 256


def iota2(shape, axis):
    return lax.broadcasted_iota(jnp.int32, shape, axis)


def three_rows(row):
    row = row.reshape(1, -1)
    high = row.astype(BF16).astype(F32)
    rest = row - high
    mid = rest.astype(BF16).astype(F32)
    low = rest - mid
    index = iota2((PAIR, row.shape[1]), 0)
    zero = jnp.zeros((PAIR, row.shape[1]), F32)
    out = jnp.where(index == 0, high, zero)
    out = jnp.where(index == 1, mid, out)
    out = jnp.where(index == 2, low, out)
    return out.astype(BF16)


def across(rows16, select):
    return lax.dot_general(rows16, select, (((0,), (0,)), ((), ())), preferred_element_type=F32)


def halves_silu(pre):
    y = pre.astype(BF16)
    return y + y * jnp.tanh(y)


def kernel(
    n,
    n_space,
    fields,
    zones,
    diff,
    rate,
    w_in,
    b_in,
    w_mid,
    b_mid,
    w_out,
    b_out,
    out,
    states,
    coef,
    face_d,
    face_e,
    rdiag,
    halo_out,
    halo_in,
    sbuf,
    xbuf,
    rbuf,
    ret,
    w1,
    w2,
    w3,
    rate_row,
    rate_col,
    halo_ssem,
    halo_rsem,
    ssem,
    rsem,
    rssem,
    rrsem,
    lsem,
    rlsem,
):
    per, rows, columns = fields.shape
    src, s3 = states.at[0], states.at[SWEEPS]
    parts = SUB // per
    width = columns // parts
    variants = 2 * parts
    lanes_at_once, lanes_step = block_lanes(width)
    hid = w_mid.shape[0]
    chunks = rows // (2 * n)
    chunk_rows = rows // chunks
    groups = rows // SUB
    here = lax.axis_index("space")
    me = lax.axis_index("field")
    has_up = here > 0
    has_down = here < n_space - 1

    barrier = pltpu.get_barrier_semaphore()
    for off in range(1, n):
        pl.semaphore_signal(
            barrier, inc=1, device_id={"field": lax.rem(me + off, n)}, device_id_type=MESH
        )

    @pl.when(has_up)
    def _():
        pl.semaphore_signal(barrier, inc=1, device_id={"space": here - 1}, device_id_type=MESH)

    @pl.when(has_down)
    def _():
        pl.semaphore_signal(barrier, inc=1, device_id={"space": here + 1}, device_id_type=MESH)

    def prep(g):
        row0 = pl.multiple_of(g * SUB, SUB)
        there = pl.ds(pl.multiple_of((row0 + HALO) * SUB, SUB), SUB * SUB)

        def lane_block(j, carry):
            at = pl.multiple_of(j * STEP, STEP)
            coefs, values = [], []
            for p in range(parts):
                cols = pl.ds(pl.multiple_of(at + p * width, STEP), STEP)
                zone = zones[pl.ds(row0, SUB), cols]
                for f in range(per):
                    value = jnp.full(zone.shape, diff[f, 0], F32)
                    for z in range(1, diff.shape[1]):
                        value = jnp.where(zone == z, diff[f, z], value)
                    coefs.append(value)
                    values.append(fields[f, pl.ds(row0, SUB), cols])
            for buf, made in ((coef, coefs), (src, values)):
                turned = jnp.swapaxes(jnp.stack(made, 0), 0, 1)
                buf[there, pl.ds(at, STEP)] = turned.reshape(SUB * SUB, STEP)
            return carry

        lax.fori_loop(0, width // STEP, lane_block, 0)

    def prep_end(i, carry):
        prep(i * (groups - 1))
        return carry

    lax.fori_loop(0, 2, prep_end, 0)
    top = HALO * SUB
    for side, row in ((0, HALO), (1, rows)):
        halo_out[side] = jnp.concatenate(
            [src[row * SUB : row * SUB + top, :], coef[row * SUB : row * SUB + top, :]], 0
        ).astype(BF16)
    heard = (n - 1) + has_up.astype(jnp.int32) + has_down.astype(jnp.int32)
    pl.semaphore_wait(barrier, heard)

    def halo_copy(side):
        target = here - 1 if side == 0 else here + 1
        return pltpu.make_async_remote_copy(
            src_ref=halo_out.at[side],
            dst_ref=halo_in.at[1 - side],
            send_sem=halo_ssem.at[side],
            recv_sem=halo_rsem.at[1 - side],
            device_id={"space": target},
            device_id_type=MESH,
        )

    @pl.when(has_up)
    def _():
        halo_copy(0).start()

    @pl.when(has_down)
    def _():
        halo_copy(1).start()

    def prep_mid(g, carry):
        prep(g)
        return carry

    lax.fori_loop(1, groups - 1, prep_mid, 0)

    lane0 = iota2((SUB, 128), 1) == 0
    lane_last = iota2((SUB, 128), 1) == 127

    def from_east(x):
        rolled = pltpu.roll(x, width - 1, 1)
        tail = rolled[:, width - 128 :]
        tail = jnp.where(lane_last, pltpu.roll(tail, SUB - per, 0), tail)
        return jnp.concatenate([rolled[:, : width - 128], tail], 1)

    def from_west(x):
        rolled = pltpu.roll(x, 1, 1)
        head = rolled[:, :128]
        head = jnp.where(lane0, pltpu.roll(head, per, 0), head)
        return jnp.concatenate([head, rolled[:, 128:]], 1)

    def at_row(r):
        return pl.ds(pl.multiple_of(r * SUB, SUB), SUB)

    def face_row(r, carry):
        a, b, c = at_row(r - 1), at_row(r), at_row(r + 1)
        mine = coef[b, :]
        down = 0.5 * (mine + coef[c, :])
        up = 0.5 * (mine + coef[a, :])
        east = 0.5 * (mine + from_east(mine))
        west = from_west(east)
        outside = jnp.logical_or(
            jnp.logical_and(r < HALO, jnp.logical_not(has_up)),
            jnp.logical_and(r >= rows + HALO, jnp.logical_not(has_down)),
        )
        scale = jnp.where(outside, 0.0, 1.0).astype(F32)
        face_d[b, :] = down
        face_e[b, :] = east
        rdiag[b, :] = scale / (1.0 + down + up + east + west)
        return carry

    def sweep_row(sweep, weight, r, carry):
        a, b, c = at_row(r - 1), at_row(r), at_row(r + 1)
        v = states[sweep, b, :]
        east = face_e[b, :]
        total = src[b, :] + face_d[b, :] * states[sweep, c, :] + face_d[a, :] * states[sweep, a, :]
        total = total + east * from_east(v) + from_west(east * v)
        states[sweep + 1, b, :] = (1.0 - weight) * v + (weight * rdiag[b, :]) * total
        return carry

    done = [set() for _ in range(SWEEPS)]
    faced = set()

    def faces(need):
        need = sorted(set(need) - faced)
        faced.update(need)
        for start in [r for r in need if r - 1 not in need]:
            stop = start
            while stop in need:
                stop += 1
            lax.fori_loop(start, stop, face_row, 0)

    def bounds(k):
        return k * chunk_rows + HALO, (k + 1) * chunk_rows + HALO

    def sweep_rows(k, sweep):
        low, high = bounds(k)
        grow = SWEEPS - 1 - sweep
        need = sorted(set(range(low - grow, high + grow)) - done[sweep])
        done[sweep].update(need)
        return need

    def stencil(k):
        low, high = bounds(k)
        lowest = max(low - SWEEPS, 0)
        faces(range(lowest if lowest > 0 else 1, min(high + SWEEPS, rows + 2 * HALO - 1)))
        for sweep in range(SWEEPS):
            need = sweep_rows(k, sweep)
            step = functools.partial(sweep_row, sweep, RELAX_WEIGHTS[sweep])
            lax.fori_loop(need[0], need[-1] + 1, step, 0)
        send(k)

    def send(k):
        low = bounds(k)[0]
        for d in range(n):
            row = (low + 2 * d) * SUB
            sbuf[k, d] = s3[row : row + PAIR, :].astype(BF16)
        for c in sends(k):
            c.start()

    def all_copies(src_buf, dst_buf, k, send_sem, recv_sem, local_sem, cols=slice(None)):
        copies = []
        for off in range(1, n):
            peer = lax.rem(me + off, n)
            copies.append(
                pltpu.make_async_remote_copy(
                    src_ref=src_buf.at[k, peer, :, cols],
                    dst_ref=dst_buf.at[k, me, :, cols],
                    send_sem=send_sem.at[k, off],
                    recv_sem=recv_sem.at[k, off],
                    device_id={"field": peer},
                    device_id_type=MESH,
                )
            )
        local = pltpu.make_async_copy(
            src_buf.at[k, me, :, cols], dst_buf.at[k, me, :, cols], local_sem.at[k]
        )
        return copies + [local]

    def sends(k):
        return all_copies(sbuf, xbuf, k, ssem, rsem, lsem)

    def returns(k, cols=slice(None)):
        return all_copies(rbuf, ret, k, rssem, rrsem, rlsem, cols)

    def halo_wait():
        for slot, row, has in ((0, 0, has_up), (1, rows + HALO, has_down)):
            there = pl.ds(row * SUB, top)

            @pl.when(has)
            def _():
                copy = halo_copy(1 - slot)
                copy.wait_recv()
                both = halo_in[slot].astype(F32)
                src[there, :] = both[:top]
                coef[there, :] = both[top:]

            @pl.when(jnp.logical_not(has))
            def _():
                src[there, :] = jnp.zeros((top, width), F32)
                coef[there, :] = jnp.zeros((top, width), F32)

        @pl.when(has_up)
        def _():
            halo_copy(0).wait_send()

        @pl.when(has_down)
        def _():
            halo_copy(1).wait_send()

        face_d[0:SUB, :] = 0.5 * (coef[0:SUB, :] + coef[SUB : 2 * SUB, :])

    def weights():
        depth = (n + 1) * PAIR
        bias = three_rows(0.5 * b_in[...])
        row, col = iota2((PAIR, depth), 0), iota2((PAIR, depth), 1)
        bias_cols = across(bias, (col == row + n * PAIR).astype(BF16))
        for v in range(variants):
            place = (row // per) * PAIR + v * per + lax.rem(row, per)
            pick = jnp.where(col == place, 0.5, 0.0).astype(BF16)
            spread = across(w_in[...], pick)
            w1[v * hid : (v + 1) * hid, :] = (spread + bias_cols).astype(BF16)
        square = (iota2((PAIR, PAIR), 0) == iota2((PAIR, PAIR), 1)).astype(BF16)
        w2[:, :hid] = w_mid[...] * jnp.asarray(0.5, BF16)
        w2[:, hid:] = across(three_rows(0.5 * b_mid[...]), square).astype(BF16)
        w3[:, :hid] = w_out[...]
        w3[:, hid:] = across(three_rows(b_out[...]), square).astype(BF16)
        rate_row[...] = jnp.zeros(rate_row.shape, F32)
        rate_row[0:1, 0 : FIELDS - 1] = rate[...].reshape(1, FIELDS - 1)
        ones = jnp.ones((PAIR, lanes_at_once), BF16)
        rate_col[...] = across(three_rows(rate_row[0:1, :])[:, :FIELDS], ones)
        for k in range(chunks):
            xbuf[k, n] = jnp.ones((PAIR, width), BF16)

    def surrogate(k, beside=None):
        ones = jnp.ones((PAIR, lanes_at_once), BF16)
        for c in sends(k):
            c.wait()

        def block(j, carry):
            start = pl.multiple_of(j * lanes_step, lanes_step)
            subs = lanes_step // lanes_at_once
            units = [(sub, v) for sub in range(subs) for v in range(variants)]
            lanes = [
                pl.ds(pl.multiple_of(start + sub * lanes_at_once, lanes_at_once), lanes_at_once)
                for sub in range(subs)
            ]
            x = [xbuf[k, :, :, at].reshape((n + 1) * PAIR, lanes_at_once) for at in lanes]
            heat_in = [xbuf[k, n - 1, :, at].astype(F32) for at in lanes]
            first, second, scaled = {}, {}, []

            def enter(sub):
                every = jnp.dot(w1[...], x[sub], preferred_element_type=F32)
                for v in range(variants):
                    first[sub * variants + v] = every[v * hid : (v + 1) * hid]

            def middle(u):
                hidden = jnp.concatenate([halves_silu(first.pop(u)), ones], 0)
                second[u] = jnp.dot(w2[...], hidden, preferred_element_type=F32)

            def leave(u):
                sub, v = units[u]
                hidden = jnp.concatenate([halves_silu(second.pop(u)), ones], 0)
                change = jnp.dot(w3[...], hidden, preferred_element_type=F32)
                last = v * per + per - 1
                heat = heat_in[sub][last : last + 1] + change[FIELDS - 1 :]
                scaled.append(change * jnp.exp(rate_col[...] * jnp.tanh(heat)))
                if v == variants - 1:
                    for s in range(n):
                        pieces = [one[s * per : (s + 1) * per] for one in scaled]
                        rbuf[k, s, :, lanes[sub]] = jnp.concatenate(pieces, 0).astype(BF16)
                    scaled.clear()

            enter(0)
            for u in range(len(units)):
                if units[u][1] == variants // 2 and units[u][0] + 1 < subs:
                    enter(units[u][0] + 1)
                middle(u)
                if beside is not None:
                    beside(j, u)
                if u > 0:
                    leave(u - 1)
            leave(len(units) - 1)
            for c in returns(k, pl.ds(start, lanes_step)):
                c.start()
            return carry

        lax.fori_loop(0, width // lanes_step, block, 0)

    def finish(k):
        for c in returns(k):
            c.wait()
        low = k * chunk_rows + HALO
        for d in range(n):
            row = (low + 2 * d) * SUB
            s3[row : row + PAIR, :] = s3[row : row + PAIR, :] + ret[k, d].astype(F32)
        for g in range(k * chunk_rows // SUB, (k + 1) * chunk_rows // SUB):

            def lane_block(j, carry, g=g):
                at = pl.multiple_of(j * STEP, STEP)
                slab = s3[(g * SUB + HALO) * SUB : ((g + 1) * SUB + HALO) * SUB, pl.ds(at, STEP)]
                turned = jnp.swapaxes(slab.reshape(SUB, SUB, STEP), 0, 1)
                for p in range(parts):
                    cols = pl.ds(pl.multiple_of(at + p * width, STEP), STEP)
                    for f in range(per):
                        out[f, pl.ds(g * SUB, SUB), cols] = turned[p * per + f]
                return carry

            lax.fori_loop(0, width // STEP, lane_block, 0)

    inner = list(range(1, chunks - 1))
    edge = [k for k in range(chunks) if k not in inner]
    order = inner + edge
    units = lanes_step // lanes_at_once * variants
    hosted = len(inner) == 2 and width // lanes_step == SWEEPS and chunk_rows == units
    for k in inner:
        stencil(k)
    weights()
    if hosted:
        surrogate(order[0])
    halo_wait()
    if not hosted:
        for k in edge:
            stencil(k)
        for i, k in enumerate(order):
            surrogate(k)
            if i > 0:
                finish(order[i - 1])
        finish(order[-1])
        return

    for k in edge:
        low, high = bounds(k)
        faces(range(max(low - 2, 1), min(high + 2, rows + 2 * HALO - 1)))

    def beside(k):
        starts = [sweep_rows(k, sweep) for sweep in range(SWEEPS)]
        stride = starts[1][0] - starts[0][0]
        start = starts[0][0]

        def row(j, u):
            weight = jnp.where(j == 0, RELAX_WEIGHTS[0], RELAX_WEIGHTS[1])
            weight = jnp.where(j == 2, RELAX_WEIGHTS[2], weight).astype(F32)
            sweep_row(j, weight, start + stride * j + u, 0)

        return row

    stencil(edge[0])
    for i, k in enumerate(order[1:]):
        surrogate(k, beside(edge[1]) if i == 0 else None)
        if i == 0:
            send(edge[1])
        finish(order[i])
    finish(order[-1])


def on_device(
    n,
    n_space,
    fields,
    zone_ids,
    diffusivity,
    heat_rate,
    weight_in,
    bias_in,
    weight_mid,
    bias_mid,
    weight_out,
    bias_out,
):
    per, rows, columns = fields.shape
    width = columns * per // SUB
    variants = 2 * SUB // per
    lanes_at_once, lanes_step = block_lanes(width)
    hid = weight_mid.shape[0]
    chunks = rows // (2 * n)
    padded = (rows + 2 * HALO) * SUB
    vmem = pl.BlockSpec(memory_space=pltpu.VMEM)
    smem = pl.BlockSpec(memory_space=pltpu.SMEM)
    slab = pltpu.VMEM((padded, width), F32)
    dma = pltpu.SemaphoreType.DMA
    return pl.pallas_call(
        functools.partial(kernel, n, n_space),
        out_shape=jax.ShapeDtypeStruct(fields.shape, F32),
        in_specs=[vmem, vmem, smem] + [vmem] * 7,
        out_specs=vmem,
        scratch_shapes=[pltpu.VMEM((SWEEPS + 1, padded, width), F32)]
        + [slab] * 4
        + [
            pltpu.VMEM((2, 2 * HALO * SUB, width), BF16),
            pltpu.VMEM((2, 2 * HALO * SUB, width), BF16),
            pltpu.VMEM((chunks, n, PAIR, width), BF16),
            pltpu.VMEM((chunks, n + 1, PAIR, width), BF16),
            pltpu.VMEM((chunks, n, PAIR, width), BF16),
            pltpu.VMEM((chunks, n, PAIR, width), BF16),
            pltpu.VMEM((variants * hid, (n + 1) * PAIR), BF16),
            pltpu.VMEM((hid, hid + PAIR), BF16),
            pltpu.VMEM((FIELDS, hid + PAIR), BF16),
            pltpu.VMEM((SUB, 128), F32),
            pltpu.VMEM((FIELDS, lanes_at_once), F32),
            dma((2,)),
            dma((2,)),
            dma((chunks, n)),
            dma((chunks, n)),
            dma((chunks, n)),
            dma((chunks, n)),
            dma((chunks,)),
            dma((chunks,)),
        ],
        compiler_params=pltpu.CompilerParams(
            collective_id=0, has_side_effects=True, vmem_limit_bytes=60 * 1024 * 1024
        ),
        cost_estimate=pl.CostEstimate(
            flops=2 * per * rows * columns // n * hid * (hid + 2 * FIELDS),
            bytes_accessed=9 * per * rows * columns,
            transcendentals=0,
        ),
    )(
        fields,
        zone_ids,
        diffusivity,
        heat_rate,
        weight_in.T,
        bias_in,
        weight_mid,
        bias_mid,
        weight_out,
        bias_out,
    )


def solution(mesh):
    n, n_space = mesh.shape["field"], mesh.shape["space"]
    return jax.shard_map(
        functools.partial(on_device, n, n_space),
        mesh=mesh,
        in_specs=(
            P("field", "space", None),
            P("space", None),
            P("field", None),
            P(),
            P(),
            P(),
            P(),
            P(),
            P(),
            P(),
        ),
        out_specs=P("field", "space", None),
        check_vma=False,
    )
```

```python
import functools

import jax
import jax.numpy as jnp
from jax import lax
from jax.experimental import pallas as pl
from jax.experimental.pallas import tpu as pltpu
from jax.sharding import PartitionSpec as P

FIELDS = 16
SWEEPS = 3
HALO = 3
SUB = 8
PAIR = 16
STEP = 256
RELAX_WEIGHTS = (0.8, 1.25, 0.95)
MESH = pl.DeviceIdType.MESH
F32 = jnp.float32
BF16 = jnp.bfloat16


def block_lanes(width):
    for once, step in ((512, 1024), (512, 512), (256, 768)):
        if width % step == 0:
            return once, step
    return 256, 256


def iota2(shape, axis):
    return lax.broadcasted_iota(jnp.int32, shape, axis)


def three_rows(row):
    row = row.reshape(1, -1)
    high = row.astype(BF16).astype(F32)
    rest = row - high
    mid = rest.astype(BF16).astype(F32)
    low = rest - mid
    index = iota2((PAIR, row.shape[1]), 0)
    zero = jnp.zeros((PAIR, row.shape[1]), F32)
    out = jnp.where(index == 0, high, zero)
    out = jnp.where(index == 1, mid, out)
    out = jnp.where(index == 2, low, out)
    return out.astype(BF16)


def across(rows16, select):
    return lax.dot_general(rows16, select, (((0,), (0,)), ((), ())), preferred_element_type=F32)


def halves_silu(pre):
    y = pre.astype(BF16)
    return y + y * jnp.tanh(y)


def kernel(
    n,
    n_space,
    fields,
    zones,
    diff,
    rate,
    w_in,
    b_in,
    w_mid,
    b_mid,
    w_out,
    b_out,
    out,
    states,
    coef,
    face_d,
    face_e,
    rdiag,
    halo_out,
    halo_in,
    sbuf,
    xbuf,
    rbuf,
    ret,
    w1,
    w2,
    w3,
    rate_row,
    rate_col,
    halo_ssem,
    halo_rsem,
    ssem,
    rsem,
    rssem,
    rrsem,
    lsem,
    rlsem,
):
    per, rows, columns = fields.shape
    src, s3 = states.at[0], states.at[SWEEPS]
    parts = SUB // per
    width = columns // parts
    variants = 2 * parts
    lanes_at_once, lanes_step = block_lanes(width)
    hid = w_mid.shape[0]
    chunks = rows // (2 * n)
    chunk_rows = rows // chunks
    groups = rows // SUB
    here = lax.axis_index("space")
    me = lax.axis_index("field")
    has_up = here > 0
    has_down = here < n_space - 1

    barrier = pltpu.get_barrier_semaphore()
    for off in range(1, n):
        pl.semaphore_signal(
            barrier, inc=1, device_id={"field": lax.rem(me + off, n)}, device_id_type=MESH
        )

    @pl.when(has_up)
    def _():
        pl.semaphore_signal(barrier, inc=1, device_id={"space": here - 1}, device_id_type=MESH)

    @pl.when(has_down)
    def _():
        pl.semaphore_signal(barrier, inc=1, device_id={"space": here + 1}, device_id_type=MESH)

    def prep(g):
        row0 = pl.multiple_of(g * SUB, SUB)
        there = pl.ds(pl.multiple_of((row0 + HALO) * SUB, SUB), SUB * SUB)

        def lane_block(j, carry):
            at = pl.multiple_of(j * STEP, STEP)
            coefs, values = [], []
            for p in range(parts):
                cols = pl.ds(pl.multiple_of(at + p * width, STEP), STEP)
                zone = zones[pl.ds(row0, SUB), cols]
                for f in range(per):
                    value = jnp.full(zone.shape, diff[f, 0], F32)
                    for z in range(1, diff.shape[1]):
                        value = jnp.where(zone == z, diff[f, z], value)
                    coefs.append(value)
                    values.append(fields[f, pl.ds(row0, SUB), cols])
            for buf, made in ((coef, coefs), (src, values)):
                turned = jnp.swapaxes(jnp.stack(made, 0), 0, 1)
                buf[there, pl.ds(at, STEP)] = turned.reshape(SUB * SUB, STEP)
            return carry

        lax.fori_loop(0, width // STEP, lane_block, 0)

    def prep_end(i, carry):
        prep(i * (groups - 1))
        return carry

    lax.fori_loop(0, 2, prep_end, 0)
    top = HALO * SUB
    for side, row in ((0, HALO), (1, rows)):
        halo_out[side] = jnp.concatenate(
            [src[row * SUB : row * SUB + top, :], coef[row * SUB : row * SUB + top, :]], 0
        ).astype(BF16)
    heard = (n - 1) + has_up.astype(jnp.int32) + has_down.astype(jnp.int32)
    pl.semaphore_wait(barrier, heard)

    def halo_copy(side):
        target = here - 1 if side == 0 else here + 1
        return pltpu.make_async_remote_copy(
            src_ref=halo_out.at[side],
            dst_ref=halo_in.at[1 - side],
            send_sem=halo_ssem.at[side],
            recv_sem=halo_rsem.at[1 - side],
            device_id={"space": target},
            device_id_type=MESH,
        )

    @pl.when(has_up)
    def _():
        halo_copy(0).start()

    @pl.when(has_down)
    def _():
        halo_copy(1).start()

    def prep_mid(g, carry):
        prep(g)
        return carry

    lax.fori_loop(1, groups - 1, prep_mid, 0)

    lane0 = iota2((SUB, 128), 1) == 0
    lane_last = iota2((SUB, 128), 1) == 127

    def from_east(x):
        rolled = pltpu.roll(x, width - 1, 1)
        tail = rolled[:, width - 128 :]
        tail = jnp.where(lane_last, pltpu.roll(tail, SUB - per, 0), tail)
        return jnp.concatenate([rolled[:, : width - 128], tail], 1)

    def from_west(x):
        rolled = pltpu.roll(x, 1, 1)
        head = rolled[:, :128]
        head = jnp.where(lane0, pltpu.roll(head, per, 0), head)
        return jnp.concatenate([head, rolled[:, 128:]], 1)

    def at_row(r):
        return pl.ds(pl.multiple_of(r * SUB, SUB), SUB)

    def face_row(r, carry):
        a, b, c = at_row(r - 1), at_row(r), at_row(r + 1)
        mine = coef[b, :]
        down = 0.5 * (mine + coef[c, :])
        up = 0.5 * (mine + coef[a, :])
        east = 0.5 * (mine + from_east(mine))
        west = from_west(east)
        outside = jnp.logical_or(
            jnp.logical_and(r < HALO, jnp.logical_not(has_up)),
            jnp.logical_and(r >= rows + HALO, jnp.logical_not(has_down)),
        )
        scale = jnp.where(outside, 0.0, 1.0).astype(F32)
        face_d[b, :] = down
        face_e[b, :] = east
        rdiag[b, :] = scale / (1.0 + down + up + east + west)
        return carry

    def sweep_row(sweep, weight, r, carry):
        a, b, c = at_row(r - 1), at_row(r), at_row(r + 1)
        v = states[sweep, b, :]
        east = face_e[b, :]
        total = src[b, :] + face_d[b, :] * states[sweep, c, :] + face_d[a, :] * states[sweep, a, :]
        total = total + east * from_east(v) + from_west(east * v)
        states[sweep + 1, b, :] = (1.0 - weight) * v + (weight * rdiag[b, :]) * total
        return carry

    done = [set() for _ in range(SWEEPS)]
    faced = set()

    def faces(need):
        need = sorted(set(need) - faced)
        faced.update(need)
        for start in [r for r in need if r - 1 not in need]:
            stop = start
            while stop in need:
                stop += 1
            lax.fori_loop(start, stop, face_row, 0)

    def bounds(k):
        return k * chunk_rows + HALO, (k + 1) * chunk_rows + HALO

    def sweep_rows(k, sweep):
        low, high = bounds(k)
        grow = SWEEPS - 1 - sweep
        need = sorted(set(range(low - grow, high + grow)) - done[sweep])
        done[sweep].update(need)
        return need

    def stencil(k):
        low, high = bounds(k)
        lowest = max(low - SWEEPS, 0)
        faces(range(lowest if lowest > 0 else 1, min(high + SWEEPS, rows + 2 * HALO - 1)))
        for sweep in range(SWEEPS):
            need = sweep_rows(k, sweep)
            step = functools.partial(sweep_row, sweep, RELAX_WEIGHTS[sweep])
            lax.fori_loop(need[0], need[-1] + 1, step, 0)
        send(k)

    def send(k):
        low = bounds(k)[0]
        for d in range(n):
            row = (low + 2 * d) * SUB
            sbuf[k, d] = s3[row : row + PAIR, :].astype(BF16)
        for c in sends(k):
            c.start()

    def all_copies(src_buf, dst_buf, k, send_sem, recv_sem, local_sem, cols=slice(None)):
        copies = []
        for off in range(1, n):
            peer = lax.rem(me + off, n)
            copies.append(
                pltpu.make_async_remote_copy(
                    src_ref=src_buf.at[k, peer, :, cols],
                    dst_ref=dst_buf.at[k, me, :, cols],
                    send_sem=send_sem.at[k, off],
                    recv_sem=recv_sem.at[k, off],
                    device_id={"field": peer},
                    device_id_type=MESH,
                )
            )
        local = pltpu.make_async_copy(
            src_buf.at[k, me, :, cols], dst_buf.at[k, me, :, cols], local_sem.at[k]
        )
        return copies + [local]

    def sends(k):
        return all_copies(sbuf, xbuf, k, ssem, rsem, lsem)

    def returns(k, cols=slice(None)):
        return all_copies(rbuf, ret, k, rssem, rrsem, rlsem, cols)

    def halo_wait():
        for slot, row, has in ((0, 0, has_up), (1, rows + HALO, has_down)):
            there = pl.ds(row * SUB, top)

            @pl.when(has)
            def _():
                copy = halo_copy(1 - slot)
                copy.wait_recv()
                both = halo_in[slot].astype(F32)
                src[there, :] = both[:top]
                coef[there, :] = both[top:]

            @pl.when(jnp.logical_not(has))
            def _():
                src[there, :] = jnp.zeros((top, width), F32)
                coef[there, :] = jnp.zeros((top, width), F32)

        @pl.when(has_up)
        def _():
            halo_copy(0).wait_send()

        @pl.when(has_down)
        def _():
            halo_copy(1).wait_send()

        face_d[0:SUB, :] = 0.5 * (coef[0:SUB, :] + coef[SUB : 2 * SUB, :])

    def weights():
        depth = (n + 1) * PAIR
        bias = three_rows(0.5 * b_in[...])
        row, col = iota2((PAIR, depth), 0), iota2((PAIR, depth), 1)
        bias_cols = across(bias, (col == row + n * PAIR).astype(BF16))
        for v in range(variants):
            place = (row // per) * PAIR + v * per + lax.rem(row, per)
            pick = jnp.where(col == place, 0.5, 0.0).astype(BF16)
            spread = across(w_in[...], pick)
            w1[v * hid : (v + 1) * hid, :] = (spread + bias_cols).astype(BF16)
        square = (iota2((PAIR, PAIR), 0) == iota2((PAIR, PAIR), 1)).astype(BF16)
        w2[:, :hid] = w_mid[...] * jnp.asarray(0.5, BF16)
        w2[:, hid:] = across(three_rows(0.5 * b_mid[...]), square).astype(BF16)
        w3[:, :hid] = w_out[...]
        w3[:, hid:] = across(three_rows(b_out[...]), square).astype(BF16)
        rate_row[...] = jnp.zeros(rate_row.shape, F32)
        rate_row[0:1, 0 : FIELDS - 1] = rate[...].reshape(1, FIELDS - 1)
        ones = jnp.ones((PAIR, lanes_at_once), BF16)
        rate_col[...] = across(three_rows(rate_row[0:1, :])[:, :FIELDS], ones)
        for k in range(chunks):
            xbuf[k, n] = jnp.ones((PAIR, width), BF16)

    def surrogate(k, beside=None):
        ones = jnp.ones((PAIR, lanes_at_once), BF16)
        for c in sends(k):
            c.wait()

        def block(j, carry):
            start = pl.multiple_of(j * lanes_step, lanes_step)
            subs = lanes_step // lanes_at_once
            units = [(sub, v) for sub in range(subs) for v in range(variants)]
            lanes = [
                pl.ds(pl.multiple_of(start + sub * lanes_at_once, lanes_at_once), lanes_at_once)
                for sub in range(subs)
            ]
            x = [xbuf[k, :, :, at].reshape((n + 1) * PAIR, lanes_at_once) for at in lanes]
            heat_in = [xbuf[k, n - 1, :, at].astype(F32) for at in lanes]
            first, second, scaled = {}, {}, []

            def enter(u):
                sub, v = units[u]
                rows_v = w1[v * hid : (v + 1) * hid, :]
                first[u] = jnp.dot(rows_v, x[sub], preferred_element_type=F32)

            def middle(u):
                hidden = jnp.concatenate([halves_silu(first.pop(u)), ones], 0)
                second[u] = jnp.dot(w2[...], hidden, preferred_element_type=F32)

            def leave(u):
                sub, v = units[u]
                hidden = jnp.concatenate([halves_silu(second.pop(u)), ones], 0)
                change = jnp.dot(w3[...], hidden, preferred_element_type=F32)
                last = v * per + per - 1
                heat = heat_in[sub][last : last + 1] + change[FIELDS - 1 :]
                scaled.append(change * jnp.exp(rate_col[...] * jnp.tanh(heat)))
                if v == variants - 1:
                    for s in range(n):
                        pieces = [one[s * per : (s + 1) * per] for one in scaled]
                        rbuf[k, s, :, lanes[sub]] = jnp.concatenate(pieces, 0).astype(BF16)
                    scaled.clear()

            enter(0)
            for u in range(len(units)):
                if u + 1 < len(units):
                    enter(u + 1)
                middle(u)
                if beside is not None:
                    beside(j, u)
                if u > 0:
                    leave(u - 1)
            leave(len(units) - 1)
            for c in returns(k, pl.ds(start, lanes_step)):
                c.start()
            return carry

        lax.fori_loop(0, width // lanes_step, block, 0)

    def finish(k):
        for c in returns(k):
            c.wait()
        low = k * chunk_rows + HALO
        for d in range(n):
            row = (low + 2 * d) * SUB
            s3[row : row + PAIR, :] = s3[row : row + PAIR, :] + ret[k, d].astype(F32)
        for g in range(k * chunk_rows // SUB, (k + 1) * chunk_rows // SUB):

            def lane_block(j, carry, g=g):
                at = pl.multiple_of(j * STEP, STEP)
                slab = s3[(g * SUB + HALO) * SUB : ((g + 1) * SUB + HALO) * SUB, pl.ds(at, STEP)]
                turned = jnp.swapaxes(slab.reshape(SUB, SUB, STEP), 0, 1)
                for p in range(parts):
                    cols = pl.ds(pl.multiple_of(at + p * width, STEP), STEP)
                    for f in range(per):
                        out[f, pl.ds(g * SUB, SUB), cols] = turned[p * per + f]
                return carry

            lax.fori_loop(0, width // STEP, lane_block, 0)

    inner = list(range(1, chunks - 1))
    edge = [k for k in range(chunks) if k not in inner]
    order = inner + edge
    units = lanes_step // lanes_at_once * variants
    hosted = len(inner) == 2 and width // lanes_step == SWEEPS and chunk_rows == units
    for k in inner:
        stencil(k)
    weights()
    halo_wait()
    if not hosted:
        for k in edge:
            stencil(k)
        for i, k in enumerate(order):
            surrogate(k)
            if i > 0:
                finish(order[i - 1])
        finish(order[-1])
        return

    for k in edge:
        low, high = bounds(k)
        faces(range(max(low - 2, 1), min(high + 2, rows + 2 * HALO - 1)))

    def beside(k):
        starts = [sweep_rows(k, sweep) for sweep in range(SWEEPS)]
        stride = starts[1][0] - starts[0][0]
        start = starts[0][0]

        def row(j, u):
            weight = jnp.where(j == 0, RELAX_WEIGHTS[0], RELAX_WEIGHTS[1])
            weight = jnp.where(j == 2, RELAX_WEIGHTS[2], weight).astype(F32)
            sweep_row(j, weight, start + stride * j + u, 0)

        return row

    for i, k in enumerate(order):
        surrogate(k, beside(edge[i]) if i < len(edge) else None)
        if i < len(edge):
            send(edge[i])
        if i > 0:
            finish(order[i - 1])
    finish(order[-1])


def on_device(
    n,
    n_space,
    fields,
    zone_ids,
    diffusivity,
    heat_rate,
    weight_in,
    bias_in,
    weight_mid,
    bias_mid,
    weight_out,
    bias_out,
):
    per, rows, columns = fields.shape
    width = columns * per // SUB
    variants = 2 * SUB // per
    lanes_at_once, lanes_step = block_lanes(width)
    hid = weight_mid.shape[0]
    chunks = rows // (2 * n)
    padded = (rows + 2 * HALO) * SUB
    vmem = pl.BlockSpec(memory_space=pltpu.VMEM)
    smem = pl.BlockSpec(memory_space=pltpu.SMEM)
    slab = pltpu.VMEM((padded, width), F32)
    dma = pltpu.SemaphoreType.DMA
    return pl.pallas_call(
        functools.partial(kernel, n, n_space),
        out_shape=jax.ShapeDtypeStruct(fields.shape, F32),
        in_specs=[vmem, vmem, smem] + [vmem] * 7,
        out_specs=vmem,
        scratch_shapes=[pltpu.VMEM((SWEEPS + 1, padded, width), F32)]
        + [slab] * 4
        + [
            pltpu.VMEM((2, 2 * HALO * SUB, width), BF16),
            pltpu.VMEM((2, 2 * HALO * SUB, width), BF16),
            pltpu.VMEM((chunks, n, PAIR, width), BF16),
            pltpu.VMEM((chunks, n + 1, PAIR, width), BF16),
            pltpu.VMEM((chunks, n, PAIR, width), BF16),
            pltpu.VMEM((chunks, n, PAIR, width), BF16),
            pltpu.VMEM((variants * hid, (n + 1) * PAIR), BF16),
            pltpu.VMEM((hid, hid + PAIR), BF16),
            pltpu.VMEM((FIELDS, hid + PAIR), BF16),
            pltpu.VMEM((SUB, 128), F32),
            pltpu.VMEM((FIELDS, lanes_at_once), F32),
            dma((2,)),
            dma((2,)),
            dma((chunks, n)),
            dma((chunks, n)),
            dma((chunks, n)),
            dma((chunks, n)),
            dma((chunks,)),
            dma((chunks,)),
        ],
        compiler_params=pltpu.CompilerParams(
            collective_id=0, has_side_effects=True, vmem_limit_bytes=60 * 1024 * 1024
        ),
        cost_estimate=pl.CostEstimate(
            flops=2 * per * rows * columns // n * hid * (hid + 2 * FIELDS),
            bytes_accessed=9 * per * rows * columns,
            transcendentals=0,
        ),
    )(
        fields,
        zone_ids,
        diffusivity,
        heat_rate,
        weight_in.T,
        bias_in,
        weight_mid,
        bias_mid,
        weight_out,
        bias_out,
    )


def solution(mesh):
    n, n_space = mesh.shape["field"], mesh.shape["space"]
    return jax.shard_map(
        functools.partial(on_device, n, n_space),
        mesh=mesh,
        in_specs=(
            P("field", "space", None),
            P("space", None),
            P("field", None),
            P(),
            P(),
            P(),
            P(),
            P(),
            P(),
            P(),
        ),
        out_specs=P("field", "space", None),
        check_vma=False,
    )
```
